512 devices in a mesh: mode: 4 (over y_hi, core), space: 128 (over y_lo, z, x).
Axes of the slice: x: 4, y: 4 (y_hi: 2, y_lo: 2; y = y_hi * 2 + y_lo), z: 16, core: 2. Of those that a mesh axis runs over, the one named last changes fastest.
Arguments:
- modes: float32 [20, 4, 1024, 1024], P('mode', None, 'space'), may hold values from -6 to 6
- coefficients: float32 [4, 4, 1024, 1024], P(None, None, 'space'), may hold values from 0.3 to 3
- coupling: int32 [80, 3], replicated, may hold values from 0 to 19, as said below
- coupling_values: float32 [80], replicated, may hold values from -3 to 3, as said below
- assignment: int32 [20], replicated, may hold values from 0 to 19, each once
Outputs:
- product: float32 [20, 4, 1024, 1024], P('mode', None, 'space')
The draws below stay inside these ranges and needn't reach their ends.
Inputs may be any that keep to these rules, and one draw needn't show every extreme that they name: `coupling`: each mode stands for a multi-index of total degree at most 3 in 3 variables (which mode is which varies). Entry e < 20 is (e, e, 0). The other entries are exactly the pairs (i, j, k) whose multi-indices differ by one in variable k (k of 1 to 3), each pair listed once in each order, in an order that varies. `coupling_values`: the entries (i, j, k) and (j, i, k) carry the same value.
All inputs are finite; a program needn't handle non-finite values.
Results may differ from the reference program's by a relative error of at most 0.0003.
Values sent between devices are 32-bit elements; how exact they have to be, the bound alone decides.
A program may use at most 64 MiB of HBM per device.

```python
import math
import jax
import jax.numpy as jnp
import numpy as np
from jax import lax

MODES = 20
KTERMS = 4
PLANES = 4
NY = 1024
NX = 1024


def pair_table():
    degree_cap = 3
    indices = []
    for first in range(degree_cap + 1):
        for second in range(degree_cap + 1):
            for third in range(degree_cap + 1):
                if first + second + third <= degree_cap:
                    indices.append((first, second, third))
    pairs = []
    for lower, multi in enumerate(indices):
        for variable in range(3):
            raised = list(multi)
            raised[variable] = raised[variable] + 1
            raised = tuple(raised)
            if raised in indices:
                pairs.append((lower, indices.index(raised), variable + 1))
    return np.array(pairs, dtype=np.int32)


def shared_order(key):
    table = pair_table()
    relabel = jax.random.permutation(jax.random.fold_in(key, 101), MODES)
    order = jax.random.permutation(jax.random.fold_in(key, 102), 2 * table.shape[0])
    return (table, relabel.astype(jnp.int32), order.astype(jnp.int32))


def draw_coupling(key, part):
    table, relabel, order = shared_order(key)
    listed = jnp.asarray(table)
    pair_id = order // 2
    flip = order % 2
    lower = relabel[listed[pair_id, 0]]
    upper = relabel[listed[pair_id, 1]]
    first = jnp.where(flip == 0, lower, upper)
    second = jnp.where(flip == 0, upper, lower)
    third = listed[pair_id, 2]
    diag = jnp.arange(MODES, dtype=jnp.int32)
    first = jnp.concatenate([diag, first])
    second = jnp.concatenate([diag, second])
    third = jnp.concatenate([jnp.zeros((MODES,), jnp.int32), third])
    return jnp.stack([first, second, third], axis=1).astype(jnp.int32)


def draw_coupling_values(key, part):
    table, relabel, order = shared_order(key)
    key = jax.random.fold_in(key, 13)
    key_pair, key_diag = jax.random.split(key)
    count = table.shape[0]
    pair_values = jnp.clip(0.5 * jax.random.normal(key_pair, (count,), jnp.float32), -3.0, 3.0)
    diag_values = jnp.clip(0.5 * jax.random.normal(key_diag, (MODES,), jnp.float32), -3.0, 3.0)
    return jnp.concatenate([diag_values, pair_values[order // 2]]).astype(jnp.float32)


def block_scale(key, shape, cuts, least, top_value):
    factor_of, own = 1.0, jax.random.fold_in(key, 6)
    for dim, parts in cuts:
        heights = jnp.exp(jax.random.uniform(jax.random.fold_in(own, dim), (parts,), jnp.float32, least / len(cuts), top_value / len(cuts)))
        factor_of = factor_of * jnp.repeat(heights, shape[dim] // parts).reshape([-1 if axis == dim else 1 for axis in range(len(shape))])
    return factor_of


def normal_values(own_key, dims, scale, bound, pieces=(), kind=jnp.bfloat16):
    factor_of = block_scale(own_key, dims, pieces, -0.22, 0.18) if pieces else 1.0
    values = jax.random.normal(own_key, dims, jnp.float32) * scale * factor_of
    return jnp.minimum(jnp.maximum(values, -bound), bound).astype(kind)


def setup_inputs(seed: int = 0) -> dict:
    key_of = jax.random.split(jax.random.key(seed), 6)
    return {
        "modes": normal_values(key_of[0], (MODES, PLANES, NX, NY), 1.0, 6.0, ((0, 4), (2, 128)), jnp.float32),
        "coefficients": jnp.clip(jnp.exp(math.log(3.0) - 2.3025851 * jax.random.uniform(key_of[1], (KTERMS, PLANES, NX, NY), jnp.float32) ** block_scale(key_of[1], (KTERMS, PLANES, NX, NY), ((2, 128),), -0.2, 0.2)), 0.3, 3.0),
        "coupling": draw_coupling(jax.random.fold_in(key_of[5], 71), 0),
        "coupling_values": draw_coupling_values(jax.random.fold_in(key_of[5], 71), 0),
        "assignment": jax.random.permutation(key_of[4], MODES).astype(jnp.int32),
    }


def slot_tensor(coupling, coupling_values, assignment, modes_count, terms_count):
    width = jnp.arange(modes_count, dtype=jnp.int32)
    terms = jnp.arange(terms_count, dtype=jnp.int32)
    test_hot = (coupling[:, 0:1] == width[None, :]).astype(jnp.float32)
    trial_hot = (coupling[:, 1:2] == width[None, :]).astype(jnp.float32)
    term_hot = (coupling[:, 2:3] == terms[None, :]).astype(jnp.float32)
    dense = jnp.einsum('e,ei,ej,ek->ijk', coupling_values, test_hot, trial_hot, term_hot, precision=lax.Precision.HIGHEST)
    placed = (assignment[:, None] == width[None, :]).astype(jnp.float32)
    return jnp.einsum('ai,bj,ijk->abk', placed, placed, dense, precision=lax.Precision.HIGHEST)


def apply_terms(field_ext, coef_ext):
    lead = field_ext.ndim - 3
    widths = [(0, 0)] * lead + [(1, 1), (0, 0), (1, 1)]
    field_pad = jnp.pad(field_ext, widths)
    coef_pad = jnp.pad(coef_ext, [(0, 0), (1, 1), (0, 0), (1, 1)])
    plane_count = field_ext.shape[-3]
    row_count = field_ext.shape[-2] - 2
    col_count = field_ext.shape[-1]
    centre_field = field_pad[..., 1:plane_count + 1, 1:row_count + 1, 1:col_count + 1]
    centre_coef = coef_pad[..., 1:plane_count + 1, 1:row_count + 1, 1:col_count + 1]
    total = jnp.zeros_like(centre_coef * centre_field)
    for offset in ((1, 0, 0), (-1, 0, 0), (0, 1, 0), (0, -1, 0), (0, 0, 1), (0, 0, -1)):
        plane_at = 1 + offset[0]
        row_at = 1 + offset[1]
        col_at = 1 + offset[2]
        other_field = field_pad[..., plane_at:plane_at + plane_count, row_at:row_at + row_count, col_at:col_at + col_count]
        other_coef = coef_pad[..., plane_at:plane_at + plane_count, row_at:row_at + row_count, col_at:col_at + col_count]
        total = total + 0.5 * (centre_coef + other_coef) * (centre_field - other_field)
    return total


def reference(modes, coefficients, coupling, coupling_values, assignment):
    slots = slot_tensor(coupling, coupling_values, assignment, MODES, KTERMS)
    modes_ext = jnp.pad(modes, [(0, 0), (0, 0), (1, 1), (0, 0)])
    coef_ext = jnp.pad(coefficients, [(0, 0), (0, 0), (1, 1), (0, 0)])

    def one_mode(carry, index):
        field = lax.dynamic_index_in_dim(modes_ext, index, 0, keepdims=False)
        terms = apply_terms(field[None], coef_ext)
        weights = lax.dynamic_index_in_dim(slots, index, 1, keepdims=False)
        return carry + jnp.einsum('ak,kpxy->apxy', weights, terms, precision=lax.Precision.HIGHEST), None

    start = jnp.zeros(modes.shape, jnp.float32)
    result, unused = lax.scan(one_mode, start, jnp.arange(MODES, dtype=jnp.int32))
    return result
```

```python
import functools

import jax
import jax.numpy as jnp
from jax import lax
from jax.experimental import pallas as pl
from jax.experimental.pallas import tpu as pltpu
from jax.sharding import PartitionSpec as P

MESH = pl.DeviceIdType.MESH
EVENS = 7
SLOTS = 20
GROUP = 5
CHIP = 10
TERMS = 4
ENTRIES = 80


def tables(high, core, coupling, values, assignment):
    i32 = jnp.int32
    rows, lanes = ENTRIES, 128
    lane = lax.broadcasted_iota(i32, (rows, lanes), 1)
    sub = lax.broadcasted_iota(i32, (rows, lanes), 0)
    slot = lane[0:1]
    first, second, term = coupling[:, 0:1], coupling[:, 1:2], coupling[:, 2:3]
    value = jnp.sum(jnp.where(lane == sub, values, 0.0), axis=1, keepdims=True)
    real = lane < SLOTS
    hit_first = jnp.logical_and(first == assignment, real)
    hit_second = jnp.logical_and(second == assignment, real)
    joined = jnp.logical_and(hit_first, term > 0)
    degree = jnp.sum(jnp.where(joined, 1, 0), axis=0, keepdims=True)
    five = jnp.where(degree == 5, 1, 0)
    by_five = jnp.sum(jnp.where(hit_second, five, 0), axis=1, keepdims=True)
    near_five = jnp.sum(jnp.where(joined, by_five, 0), axis=0, keepdims=True)
    odd = jnp.logical_or(degree <= 2, near_five > 0)
    even = jnp.where(odd, 0, jnp.where(slot < SLOTS, 1, 0))
    lane24, sub24 = lane[:24], sub[:24]
    even_col = jnp.sum(jnp.where(lane24 == sub24, even, 0), axis=1, keepdims=True)
    ahead = jnp.sum(jnp.where(sub24 < lane24, even_col, 0), axis=0, keepdims=True)
    low = jnp.sum(jnp.where(sub24 < CHIP, even_col, 0), axis=0, keepdims=True)
    order0 = ahead
    order1 = jnp.where(slot < CHIP, ahead + (EVENS - low), ahead - low)
    mine = jnp.where(high == 0, order0, order1)
    theirs = jnp.where(high == 0, order1, order0)
    key_row = jnp.where(even > 0, mine, 99)
    key_col = jnp.sum(jnp.where(lane24 == sub24, key_row, 0), axis=1, keepdims=True)
    slot_of = jnp.sum(jnp.where(key_col == lane24, jnp.where(sub24 < SLOTS, sub24, 0), 0), axis=0, keepdims=True)
    local = slot - high * CHIP
    here = jnp.logical_and(local >= 0, local < CHIP)
    place = jnp.where(core == 0, local, jnp.where(local < GROUP, local + GROUP, local - GROUP))
    place = jnp.where(here, place, 0)
    code = slot * 4096 + theirs * 256 + place * 16 + even * 2 + jnp.where(here, 1, 0)
    code_of = jnp.sum(jnp.where(hit_second, code, 0), axis=1, keepdims=True)
    l_index, l_weight, r_index, r_weight = [], [], [], []
    for k in range(1, TERMS):
        chosen = jnp.logical_and(hit_first, term == k)
        lower = jnp.min(jnp.where(chosen, code_of, 1 << 24), axis=0, keepdims=True)
        upper = jnp.max(jnp.where(chosen, code_of, -1), axis=0, keepdims=True)
        upper = jnp.where(upper == lower, -1, upper)
        for found, there in ((lower, lower < (1 << 24)), (upper, upper >= 0)):
            weight = jnp.sum(jnp.where(jnp.logical_and(chosen, code_of == found), value, 0.0), axis=0, keepdims=True)
            is_here = (found % 2) == 1
            is_even = ((found // 2) % 2) == 1
            use_l = jnp.logical_and(there, is_here)
            use_r = jnp.logical_and(there, jnp.logical_and(is_even, jnp.logical_not(is_here)))
            l_index.append(jnp.where(use_l, (found // 16) % 16, 0))
            l_weight.append(jnp.where(use_l, weight, 0.0))
            r_index.append(jnp.where(use_r, (found // 256) % 16, 0))
            r_weight.append(jnp.where(use_r, weight, 0.0))
    diagonal = jnp.sum(jnp.where(jnp.logical_and(hit_first, term == 0), value, 0.0), axis=0, keepdims=True)
    zero_i = jnp.zeros_like(slot)
    zero_f = jnp.zeros_like(diagonal)
    theirs = jnp.where(even > 0, theirs, 0)
    ints = jnp.concatenate(l_index + r_index + [theirs, slot_of, place, zero_i], axis=0)
    floats = jnp.concatenate(l_weight + r_weight + [jnp.where(even > 0, 1.0, 0.0), diagonal, zero_f, zero_f], axis=0)
    return ints, floats


def kernel(
    spaces, sure,
    modes, coefs, coupling, values, assignment, out,
    m, c, es, er, gy, gx, gz, db, gh, ak, dh, sb, rb, hs, hr, dr, akr, acc, tiv, tfv, ti, tf,
    load_sem, table_sem, sib_s, sib_r, edge_s, edge_r, item_s, item_r, plane_s, plane_r, fwd_s, fwd_r, res_sem, res_s, res_r,
):
    f32 = jnp.float32
    mode, space = lax.axis_index("mode"), lax.axis_index("space")
    high, core = mode // 2, mode % 2
    sibling = (high * 2 + (1 - core), space)
    partner = ((1 - high) * 2 + core, space)
    has_low, has_high = space > 0, space < spaces - 1
    width = modes.shape[3]
    maybe = EVENS - sure
    groups = [list(range(maybe))[i : i + 4] for i in range(0, maybe, 4)]
    planes = (3 * core, 1 + core, 2 - core, 3 - 3 * core)

    loads = []
    for at, plane in enumerate(planes):
        loads.append(pltpu.make_async_copy(modes.at[:, pl.ds(plane, 1)], m.at[pl.ds(0, GROUP), pl.ds(at, 1)], load_sem.at[0, at]))
        loads.append(pltpu.make_async_copy(coefs.at[:, pl.ds(plane, 1)], c.at[:, pl.ds(at, 1)], load_sem.at[1, at]))
    for copy in loads:
        copy.start()

    barrier = pltpu.get_barrier_semaphore()
    for target in (sibling, partner):
        pl.semaphore_signal(barrier, inc=1, device_id=target, device_id_type=MESH)
    for there, step in ((has_low, -1), (has_high, 1)):
        @pl.when(there)
        def _():
            for who in (mode, sibling[0]):
                pl.semaphore_signal(barrier, inc=1, device_id=(who, space + step), device_id_type=MESH)

    ints, floats = tables(high, core, coupling[...], values[...], assignment[...])
    tiv[...] = ints
    tfv[...] = floats
    table_copies = [
        pltpu.make_async_copy(tiv, ti, table_sem.at[0]),
        pltpu.make_async_copy(tfv, tf, table_sem.at[1]),
    ]
    for copy in table_copies:
        copy.start()

    for copy in loads:
        copy.wait()

    for side, row in ((0, 7), (1, 0)):
        for other, held in ((0, (0, 1)), (1, (3, 2))):
            for p in range(2):
                for i in range(GROUP):
                    es[side, other, pl.ds(i * 2 + p, 1), :] = m[i, held[p], pl.ds(row, 1), :]
                for kk in range(2):
                    es[side, other, pl.ds(10 + kk * 2 + p, 1), :] = c[2 * core + kk, held[p], pl.ds(row, 1), :]

    for there, side in ((has_low, 0), (has_high, 1)):
        @pl.when(jnp.logical_not(there))
        def _():
            er[side] = jnp.zeros(er.shape[1:], f32)
            hr[side] = jnp.zeros(hr.shape[1:], f32)

    pl.semaphore_wait(barrier, 2 + 2 * has_low.astype(jnp.int32) + 2 * has_high.astype(jnp.int32))

    theirs = (3 - 3 * core, 2 - core, 1 + core)
    to_sibling = [
        pltpu.make_async_remote_copy(
            modes.at[:, pl.ds(plane, 1)], m.at[pl.ds(GROUP, GROUP), pl.ds(at, 1)],
            sib_s.at[at], sib_r.at[at], device_id=sibling, device_id_type=MESH,
        )
        for at, plane in enumerate(theirs)
    ]
    for copy in to_sibling:
        copy.start()

    def edge_copy(side, other, source):
        who = mode if other == 0 else sibling[0]
        return pltpu.make_async_remote_copy(
            es.at[side, other], er.at[side, source], edge_s.at[side, other], edge_r.at[side, source],
            device_id=(who, space + (1 if side == 0 else -1)), device_id_type=MESH,
        )

    for there, side in ((has_high, 0), (has_low, 1)):
        @pl.when(there)
        def _():
            for other in range(2):
                edge_copy(side, other, core).start()

    row = lax.broadcasted_iota(jnp.int32, (8, width), 0)
    col = lax.broadcasted_iota(jnp.int32, (8, width), 1)
    for k in range(TERMS):
        a0, a1, ah = 0.5 * c[k, 0], 0.5 * c[k, 1], 0.5 * c[k, 2]
        for p, a in ((0, a0), (1, a1)):
            gy[k, p] = jnp.where(col == 0, 0.0, a + pltpu.roll(a, 1, 1))
            gx[k, p] = jnp.where(row == 0, 0.0, a + pltpu.roll(a, 1, 0))
        side = jnp.where(jnp.logical_or(col == 0, col == width - 1), 1.0, 0.0)
        db[k, 0] = a0 * (1.0 + side)
        db[k, 1] = a1 * side
        gz[k, 0] = a0 + a1
        gz[k, 1] = a1 + ah

    def stencil(v0, v1, vh, terms, store):
        d0, d1 = v0 - v1, v1 - vh
        y0, y1 = v0 - pltpu.roll(v0, 1, 1), v1 - pltpu.roll(v1, 1, 1)
        x0, x1 = v0 - pltpu.roll(v0, 1, 0), v1 - pltpu.roll(v1, 1, 0)
        for k in terms:
            between = gz[k, 0] * d0
            f = gy[k, 0] * y0
            g = gx[k, 0] * x0
            store(k, 0, (f - pltpu.roll(f, width - 1, 1)) + (g - pltpu.roll(g, 7, 0)) + (between + db[k, 0] * v0))
            f = gy[k, 1] * y1
            g = gx[k, 1] * x1
            store(k, 1, (f - pltpu.roll(f, width - 1, 1)) + (g - pltpu.roll(g, 7, 0)) + (gz[k, 1] * d1 + db[k, 1] * v1 - between))

    def own_stencil(b, carry):
        def store(k, p, value):
            ak[b * TERMS + k, p] = value
        stencil(m[b, 0], m[b, 1], m[b, 2], range(TERMS), store)
        return carry

    lax.fori_loop(0, GROUP, own_stencil, 0)
    for copy in table_copies:
        copy.wait()
    for copy in to_sibling:
        copy.wait_recv()

    def item_copy(j):
        return pltpu.make_async_remote_copy(
            sb.at[j], rb.at[j, pl.ds(0, 2)], item_s.at[j], item_r.at[j], device_id=partner, device_id_type=MESH
        )

    def raw_place(j):
        slot = ti[13, j]
        return slot, ti[14, slot], jnp.where(slot // CHIP == high, 1.0, 0.0).astype(f32)

    for j in range(sure):
        slot, place, ours = raw_place(j)
        for p in range(2):
            sb[j, p] = m[place, p]
        item_copy(j).start()

    lax.fori_loop(GROUP, CHIP, own_stencil, 0)

    for there, side in ((has_low, 0), (has_high, 1)):
        @pl.when(there)
        def _():
            for source in range(2):
                edge_copy(side, 0, source).wait_recv()

    def tile(top0, top1, bottom0, bottom1):
        return jnp.where(row == 0, top0, jnp.where(row == 7, bottom0, jnp.where(row == 4, top1, bottom1)))

    def own_edges(v0, v1):
        return jnp.where(jnp.logical_or(row == 0, row == 7), v0, pltpu.roll(v1, 4, 0))

    def arrived(ref, lead, r):
        return [ref[(side,) + lead + (pl.ds(r + p, 1), slice(None))] for side in range(2) for p in range(2)]

    for k in range(TERMS):
        gh[k] = 0.5 * (own_edges(c[k, 0], c[k, 1]) + tile(*arrived(er, (k // 2,), 10 + (k % 2) * 2)))
    for b in range(CHIP):
        source = core if b < GROUP else 1 - core
        dh[b] = own_edges(m[b, 0], m[b, 1]) - tile(*arrived(er, (source,), (b % GROUP) * 2))

    outer = jnp.logical_or(row == 0, row == 7)

    def spread(packed):
        return jnp.where(outer, packed, 0.0), jnp.where(outer, pltpu.roll(packed, 4, 0), 0.0)

    def gathered(slot, first, applied, stride, shift, edges, scale, starts):
        total0, total1, packed = starts
        for k in range(1, TERMS):
            along = None
            for side in range(2):
                at = first + (k - 1) * 2 + side
                index = ti[at, slot]
                weight = tf[at, slot] * scale
                total0 = total0 + weight * applied[index * stride + (k - shift), 0]
                total1 = total1 + weight * applied[index * stride + (k - shift), 1]
                part = weight * edges[index]
                along = part if along is None else along + part
            packed = gh[k] * along if packed is None else packed + gh[k] * along
        edge0, edge1 = spread(packed)
        return total0 + edge0, total1 + edge1

    for j in range(sure, EVENS):
        slot, place, ours = raw_place(j)
        starts = (ours * m[place, 0], ours * m[place, 1], None)
        sb[j, 0], sb[j, 1] = gathered(slot, 0, ak, TERMS, 0, dh, 1.0 - ours, starts)
        item_copy(j).start()

    def slot_at(b):
        return high * CHIP + jnp.where(b < GROUP, core * GROUP + b, (1 - core) * GROUP + b - GROUP)

    def local_sum(b, carry):
        slot = slot_at(b)
        weight = tf[13, slot]
        starts = (weight * ak[b * TERMS, 0], weight * ak[b * TERMS, 1], gh[0] * (weight * dh[b]))
        acc[b, 0], acc[b, 1] = gathered(slot, 0, ak, TERMS, 0, dh, 1.0, starts)
        return carry

    lax.fori_loop(0, CHIP, local_sum, 0)

    def plane_copy(j):
        return pltpu.make_async_remote_copy(
            rb.at[j, pl.ds(1, 1)], rb.at[j, pl.ds(2, 1)], plane_s.at[j], plane_r.at[j], device_id=sibling, device_id_type=MESH
        )

    def edge_on(side, g):
        return pltpu.make_async_remote_copy(
            hs.at[side, g], hr.at[side, g], fwd_s.at[side, g], fwd_r.at[side, g],
            device_id=(mode, space + (1 if side == 0 else -1)), device_id_type=MESH,
        )

    for g, members in enumerate(groups):
        for n, j in enumerate(members):
            item_copy(j).wait_recv()
            plane_copy(j).start()
            for side, r in ((0, 7), (1, 0)):
                for p in range(2):
                    hs[side, g, pl.ds(n * 2 + p, 1), :] = rb[j, p, pl.ds(r, 1), :]
        for there, side in ((has_high, 0), (has_low, 1)):
            @pl.when(there)
            def _():
                edge_on(side, g).start()

    def raw_stencil(j, carry):
        def store(k, p, value):
            akr[j * 3 + k - 1, p] = value
        stencil(rb[j, 0], rb[j, 1], rb[j, 2], range(1, TERMS), store)
        return carry

    for g, members in enumerate(groups):
        for j in members:
            plane_copy(j).wait_recv()
        lax.fori_loop(members[0], members[-1] + 1, raw_stencil, 0)
        for there, side in ((has_low, 0), (has_high, 1)):
            @pl.when(there)
            def _():
                edge_on(side, g).wait_recv()
        for n, j in enumerate(members):
            dr[j] = own_edges(rb[j, 0], rb[j, 1]) - tile(*arrived(hr, (g,), n * 2))

    def remote_sum(b, carry):
        slot = slot_at(b)
        index = ti[12, slot]
        early = index < maybe
        weight = jnp.where(early, tf[12, slot], 0.0)
        index = jnp.where(early, index, 0)
        starts = (acc[b, 0] + weight * rb[index, 0], acc[b, 1] + weight * rb[index, 1], None)
        acc[b, 0], acc[b, 1] = gathered(slot, 6, akr, 3, 1, dr, 1.0, starts)
        return carry

    lax.fori_loop(0, CHIP, remote_sum, 0)

    results = [
        pltpu.make_async_remote_copy(
            acc.at[pl.ds(GROUP, GROUP), pl.ds(p, 1)], out.at[:, pl.ds(planes[p], 1)], res_s.at[p], res_r.at[p],
            device_id=sibling, device_id_type=MESH,
        )
        for p in range(2)
    ] + [
        pltpu.make_async_copy(acc.at[pl.ds(0, GROUP), pl.ds(p, 1)], out.at[:, pl.ds(planes[p], 1)], res_sem.at[p])
        for p in range(2)
    ]
    for copy in results:
        copy.start()

    for copy in to_sibling:
        copy.wait_send()
    for there, side in ((has_high, 0), (has_low, 1)):
        @pl.when(there)
        def _():
            for other in range(2):
                edge_copy(side, other, core).wait_send()
            for g in range(len(groups)):
                edge_on(side, g).wait_send()
    for j in range(EVENS):
        item_copy(j).wait_send()
    for j in range(maybe):
        plane_copy(j).wait_send()
    for p in range(2):
        results[p].wait_send()
        results[2 + p].wait()
        pltpu.make_async_remote_copy(
            acc.at[pl.ds(GROUP, GROUP), pl.ds(p, 1)], out.at[:, pl.ds(theirs[p], 1)], res_s.at[p], res_r.at[p],
            device_id=sibling, device_id_type=MESH,
        ).wait_recv()


def galerkin(spaces, sure, collective, modes, coefs, coupling, values, assignment):
    width = modes.shape[3]
    f32 = jnp.float32
    maybe = EVENS - sure
    groups = -(-maybe // 4)
    dma = pltpu.SemaphoreType.DMA
    vmem = pltpu.VMEM
    scratch = [
        vmem((CHIP, 4, 8, width), f32),
        vmem((TERMS, 4, 8, width), f32),
        vmem((2, 2, 16, width), f32),
        vmem((2, 2, 16, width), f32),
        vmem((TERMS, 2, 8, width), f32),
        vmem((TERMS, 2, 8, width), f32),
        vmem((TERMS, 2, 8, width), f32),
        vmem((TERMS, 2, 8, width), f32),
        vmem((TERMS, 8, width), f32),
        vmem((CHIP * TERMS, 2, 8, width), f32),
        vmem((CHIP, 8, width), f32),
        vmem((EVENS, 2, 8, width), f32),
        vmem((EVENS, 3, 8, width), f32),
        vmem((2, groups, 8, width), f32),
        vmem((2, groups, 8, width), f32),
        vmem((maybe, 8, width), f32),
        vmem((maybe * 3, 2, 8, width), f32),
        vmem((CHIP, 2, 8, width), f32),
        vmem((16, 128), jnp.int32),
        vmem((16, 128), f32),
        pltpu.SMEM((16, 128), jnp.int32),
        pltpu.SMEM((16, 128), f32),
        dma((2, 4)), dma((2,)), dma((3,)), dma((3,)), dma((2, 2)), dma((2, 2)), dma((EVENS,)), dma((EVENS,)),
        dma((maybe,)), dma((maybe,)), dma((2, groups)), dma((2, groups)), dma((2,)), dma((2,)), dma((2,)),
    ]
    anywhere = pl.BlockSpec(memory_space=pl.ANY)
    held = pl.BlockSpec(memory_space=pltpu.VMEM)
    return pl.pallas_call(
        functools.partial(kernel, spaces, sure),
        out_shape=jax.ShapeDtypeStruct(modes.shape, f32),
        in_specs=[anywhere, anywhere, held, held, held],
        out_specs=anywhere,
        scratch_shapes=scratch,
        compiler_params=pltpu.CompilerParams(
            collective_id=collective, has_side_effects=True, vmem_limit_bytes=32 * 1024 * 1024
        ),
        name="galerkin",
    )(modes, coefs, coupling, values, assignment)


def solution(mesh):
    spaces = mesh.shape["space"]

    def shards(modes, coefficients, coupling, coupling_values, assignment):
        pad = 128 - assignment.shape[0]
        values = jnp.pad(coupling_values, (0, 128 - coupling_values.shape[0]))[None]
        held = jnp.pad(assignment, (0, pad), constant_values=-1)[None]
        return galerkin(spaces, 0, 0, modes, coefficients, coupling, values, held)

    in_specs = (P("mode", None, "space", None), P(None, None, "space", None), P(), P(), P())
    out_specs = P("mode", None, "space", None)
    return jax.shard_map(shards, mesh=mesh, in_specs=in_specs, out_specs=out_specs, check_vma=False)
```

```python
import functools

import jax
import jax.numpy as jnp
from jax import lax
from jax.experimental import pallas as pl
from jax.experimental.pallas import tpu as pltpu
from jax.sharding import PartitionSpec as P

MESH = pl.DeviceIdType.MESH
EVENS = 7
SLOTS = 20
GROUP = 5
CHIP = 10
TERMS = 4
ENTRIES = 80
EARLY = 2
LATE = EVENS - 2
ENDS = EVENS - LATE
INF = 1 << 24


def tables(high, core, coupling, values, assignment):
    i32 = jnp.int32
    slot = lax.broadcasted_iota(i32, (1, SLOTS), 1)
    lane = lax.broadcasted_iota(i32, (SLOTS, SLOTS), 1)
    sub = lax.broadcasted_iota(i32, (SLOTS, SLOTS), 0)
    eye = lax.broadcasted_iota(i32, (ENTRIES, ENTRIES), 0) == lax.broadcasted_iota(i32, (ENTRIES, ENTRIES), 1)
    first, second, term = [jnp.sum(jnp.where(eye, coupling[n : n + 1], 0), axis=1, keepdims=True) for n in range(3)]
    value = jnp.sum(jnp.where(eye, values, 0.0), axis=1, keepdims=True)
    hit_first = first == assignment
    hit_second = second == assignment
    joined = jnp.logical_and(hit_first, term > 0)
    degree = jnp.sum(jnp.where(joined, 1, 0), axis=0, keepdims=True)
    five = jnp.where(degree == 5, 1, 0)
    by_five = jnp.sum(jnp.where(hit_second, five, 0), axis=1, keepdims=True)
    near_five = jnp.sum(jnp.where(joined, by_five, 0), axis=0, keepdims=True)
    even = jnp.where(jnp.logical_or(degree <= 2, near_five > 0), 0, 1)
    even_col = jnp.sum(jnp.where(lane == sub, even, 0), axis=1, keepdims=True)
    ahead = jnp.sum(jnp.where(sub < lane, even_col, 0), axis=0, keepdims=True)
    low = jnp.sum(jnp.where(sub < CHIP, even_col, 0), axis=0, keepdims=True)
    order0 = ahead
    order1 = jnp.where(slot < CHIP, ahead + (EVENS - low), ahead - low)
    mine = jnp.where(high == 0, order0, order1)
    theirs = jnp.where(high == 0, order1, order0)
    key_row = jnp.where(even > 0, mine, 99)
    key_col = jnp.sum(jnp.where(lane == sub, key_row, 0), axis=1, keepdims=True)
    slot_of = jnp.sum(jnp.where(key_col == lane, sub, 0), axis=0, keepdims=True)
    local = slot - high * CHIP
    here = jnp.logical_and(local >= 0, local < CHIP)
    place = jnp.where(core == 0, local, jnp.where(local < GROUP, local + GROUP, local - GROUP))
    place = jnp.where(here, place, CHIP + slot - (1 - high) * CHIP)
    code = slot * 8192 + theirs * 512 + place * 16 + even * 2 + jnp.where(here, 1, 0)
    code_of = jnp.sum(jnp.where(hit_second, code, 0), axis=1, keepdims=True)
    l_index, l_weight, r_index, r_weight, a_index, a_weight = [], [], [], [], [], []
    for k in range(1, TERMS):
        chosen = jnp.logical_and(hit_first, term == k)
        lower = jnp.min(jnp.where(chosen, code_of, INF), axis=0, keepdims=True)
        upper = jnp.max(jnp.where(chosen, code_of, -1), axis=0, keepdims=True)
        upper = jnp.where(upper == lower, -1, upper)
        for found, there in ((lower, lower < INF), (upper, upper >= 0)):
            weight = jnp.sum(jnp.where(jnp.logical_and(chosen, code_of == found), value, 0.0), axis=0, keepdims=True)
            is_here = (found % 2) == 1
            is_even = ((found // 2) % 2) == 1
            use_l = jnp.logical_and(there, is_here)
            use_r = jnp.logical_and(there, jnp.logical_and(is_even, jnp.logical_not(is_here)))
            l_index.append(jnp.where(use_l, (found // 16) % 32, 0))
            l_weight.append(jnp.where(use_l, weight, 0.0))
            r_index.append(jnp.where(use_r, (found // 512) % 16, 0))
            r_weight.append(jnp.where(use_r, weight, 0.0))
            a_index.append(jnp.where(there, (found // 16) % 32, 0))
            a_weight.append(jnp.where(there, weight, 0.0))
    diagonal = jnp.sum(jnp.where(jnp.logical_and(hit_first, term == 0), value, 0.0), axis=0, keepdims=True)
    zero_i = jnp.zeros_like(slot)
    zero_f = jnp.zeros_like(diagonal)
    theirs = jnp.where(even > 0, theirs, 0)
    place = jnp.where(here, place, 0)

    def within(rows, size):
        return [jnp.clip(x, 0, size - 1) for x in rows]

    l_index, r_index, a_index = within(l_index, CHIP), within(r_index, EVENS), within(a_index, SLOTS)
    ints = within([theirs], EVENS) + within([slot_of], SLOTS) + within([place], CHIP) + [zero_i]
    floats = [jnp.where(even > 0, 1.0, 0.0), diagonal, zero_f, zero_f]
    ints = jnp.concatenate(l_index + r_index + ints + a_index + [zero_i, zero_i], axis=0)
    floats = jnp.concatenate(l_weight + r_weight + floats + a_weight + [zero_f, zero_f], axis=0)
    return ints, floats


def kernel(
    spaces,
    modes, coefs, coupling, values, assignment, out,
    m, c, es, er, gy, gx, gz, db, gh, ak, dh, sb, rb, ts, tr, hs, hr, dr, akr, acc, sh, se, ds, gs,
    rl, akl, drl, ghf, trf, drf, far,
    cv, vv, av, tiv, tfv, ti, tf,
    load_sem, small_sem, table_sem, sib_s, sib_r, edge_s, edge_r, item_s, item_r, tile_s, tile_r, plane_s, plane_r,
    fwd_s, fwd_r, seam_s, seam_r, pair_s, pair_r, outer_s, outer_r, give_s, give_r,
):
    f32, i32 = jnp.float32, jnp.int32
    mode, space = lax.axis_index("mode"), lax.axis_index("space")
    high, core = mode // 2, mode % 2
    half = spaces // 2
    low_seam, high_seam = space < 0, space < 0
    seam = jnp.logical_or(low_seam, high_seam)
    has_low = jnp.logical_and(space > 0, jnp.logical_not(low_seam))
    has_high = jnp.logical_and(space < spaces - 1, jnp.logical_not(high_seam))
    across = jnp.where(low_seam, space - 1, space + 1)
    sibling_mode = high * 2 + (1 - core)
    sibling = (sibling_mode, space)
    partner = ((1 - high) * 2 + core, space)
    diagonal = ((1 - high) * 2 + (1 - core), space)
    width = modes.shape[3]
    groups = [list(range(LATE))[i : i + 4] for i in range(0, LATE, 4)]
    planes = (3 * core, 1 + core, 2 - core, 3 - 3 * core)
    theirs = (3 - 3 * core, 2 - core, 1 + core)
    ups = ((has_high, 0), (has_low, 1))
    downs = ((has_low, 0), (has_high, 1))

    def signal(target):
        pl.semaphore_signal(barrier, inc=1, device_id=target, device_id_type=MESH)

    barrier = pltpu.get_barrier_semaphore()
    signal(sibling)
    signal(partner)
    for there, step in ((has_low, -1), (has_high, 1)):
        @pl.when(there)
        def _():
            for who in (mode, sibling_mode):
                signal((who, space + step))

    @pl.when(seam)
    def _():
        signal(diagonal)

    @pl.when(low_seam)
    def _():
        for who in range(4):
            signal((who, space - 1))

    loads = []
    for at, plane in enumerate(planes):
        loads.append(pltpu.make_async_copy(modes.at[:, pl.ds(plane, 1)], m.at[pl.ds(0, GROUP), pl.ds(at, 1)], load_sem.at[0, at]))
        loads.append(pltpu.make_async_copy(coefs.at[:, pl.ds(plane, 1)], c.at[:, pl.ds(at, 1)], load_sem.at[1, at]))
    smalls = [
        pltpu.make_async_copy(source, target, small_sem.at[n])
        for n, (source, target) in enumerate(((coupling, cv), (values, vv), (assignment, av)))
    ]
    for copy in smalls + loads:
        copy.start()

    peers = 2 + 2 * has_low.astype(i32) + 2 * has_high.astype(i32) + seam.astype(i32) + 4 * high_seam.astype(i32)
    pl.semaphore_wait(barrier, peers)

    to_sibling = [
        pltpu.make_async_remote_copy(
            modes.at[:, pl.ds(plane, 1)], m.at[pl.ds(GROUP, GROUP), pl.ds(at, 1)],
            sib_s.at[at], sib_r.at[at], device_id=sibling, device_id_type=MESH,
        )
        for at, plane in enumerate(theirs)
    ]
    for copy in to_sibling:
        copy.start()

    for copy in smalls:
        copy.wait()
    tiv[...] = jnp.zeros(tiv.shape, i32)
    tfv[...] = jnp.zeros(tfv.shape, f32)
    tiv[:, 0:SLOTS], tfv[:, 0:SLOTS] = tables(high, core, cv[...], vv[...], av[...])
    table_copies = [
        pltpu.make_async_copy(tiv, ti, table_sem.at[0]),
        pltpu.make_async_copy(tfv, tf, table_sem.at[1]),
    ]
    for copy in table_copies:
        copy.start()

    for copy in loads:
        copy.wait()

    for side, row in ((0, 7), (1, 0)):
        for other, held in ((0, (0, 1)), (1, (3, 2))):
            for p in range(2):
                for i in range(GROUP):
                    es[side, other, pl.ds(i * 2 + p, 1), :] = m[i, held[p], pl.ds(row, 1), :]
                for kk in range(2):
                    es[side, other, pl.ds(10 + kk * 2 + p, 1), :] = c[2 * core + kk, held[p], pl.ds(row, 1), :]

    def edge_copy(side, other, source):
        who = mode if other == 0 else sibling_mode
        return pltpu.make_async_remote_copy(
            es.at[side, other], er.at[side, source], edge_s.at[side, other], edge_r.at[side, source],
            device_id=(who, space + (1 if side == 0 else -1)), device_id_type=MESH,
        )

    seam_side = jnp.where(low_seam, 1, 0)

    def seam_copy(chip, other, source):
        who = chip * 2 + (core if other == 0 else 1 - core)
        return pltpu.make_async_remote_copy(
            es.at[seam_side, other], sh.at[source], seam_s.at[chip, other], seam_r.at[source],
            device_id=(who, across), device_id_type=MESH,
        )

    def pair_copy(other, source):
        return pltpu.make_async_remote_copy(
            es.at[seam_side, other], se.at[source], pair_s.at[other], pair_r.at[source],
            device_id=partner if other == 0 else diagonal, device_id_type=MESH,
        )

    @pl.when(high_seam)
    def _():
        for chip in range(2):
            for other in range(2):
                seam_copy(chip, other, mode).start()

    for there, side in ups:
        @pl.when(there)
        def _():
            for other in range(2):
                edge_copy(side, other, core).start()

    @pl.when(seam)
    def _():
        for other in range(2):
            pair_copy(other, core).start()

    for there, side in downs:
        @pl.when(jnp.logical_not(there))
        def _():
            er[side] = jnp.zeros(er.shape[1:], f32)
            hr[side] = jnp.zeros(hr.shape[1:], f32)

    row = lax.broadcasted_iota(i32, (8, width), 0)
    col = lax.broadcasted_iota(i32, (8, width), 1)

    def along_plane(k, p, carry):
        a = 0.5 * c[k, p]
        gy[k, p] = jnp.where(col == 0, 0.0, a + pltpu.roll(a, 1, 1))
        gx[k, p] = jnp.where(row == 0, 0.0, a + pltpu.roll(a, 1, 0))
        side = jnp.where(jnp.logical_or(col == 0, col == width - 1), 1.0, 0.0)
        db[k, p] = a * (side + carry)

    def near_faces(k, carry):
        along_plane(k, 0, 1.0)
        along_plane(k, 1, 0.0)
        gz[k, 0] = 0.5 * (c[k, 0] + c[k, 1])
        gz[k, 1] = 0.5 * (c[k, 1] + c[k, 2])
        return carry

    def far_faces(k, carry):
        along_plane(k, 3, 1.0)
        along_plane(k, 2, 0.0)
        gz[k, 2] = 0.5 * (c[k, 2] + c[k, 3])
        return carry

    def stencil(v, terms, store, far_side=False):
        p0, p1, z0 = (3, 2, 2) if far_side else (0, 1, 0)
        v0, v1, vh = v
        d0, d1 = v0 - v1, v1 - vh
        y0, y1 = v0 - pltpu.roll(v0, 1, 1), v1 - pltpu.roll(v1, 1, 1)
        x0, x1 = v0 - pltpu.roll(v0, 1, 0), v1 - pltpu.roll(v1, 1, 0)
        for k in terms:
            between = gz[k, z0] * d0
            f = gy[k, p0] * y0
            g = gx[k, p0] * x0
            store(k, p0, (f - pltpu.roll(f, width - 1, 1)) + (g - pltpu.roll(g, 7, 0)) + (between + db[k, p0] * v0))
            f = gy[k, p1] * y1
            g = gx[k, p1] * x1
            store(k, p1, (f - pltpu.roll(f, width - 1, 1)) + (g - pltpu.roll(g, 7, 0)) + (gz[k, 1] * d1 + db[k, p1] * v1 - between))

    def own_stencil(b, carry):
        def store(k, p, value):
            ak[b * TERMS + k, p] = value
        stencil((m[b, 0], m[b, 1], m[b, 2]), range(TERMS), store)
        return carry

    lax.fori_loop(0, TERMS, near_faces, 0)
    for copy in table_copies:
        copy.wait()
    for copy in to_sibling:
        copy.wait_recv()

    outer = jnp.logical_or(row == 0, row == 7)
    middle = jnp.logical_or(row == 3, row == 4)
    upper = jnp.logical_or(row == 0, row == 4)

    def spread(packed):
        return jnp.where(outer, packed, 0.0), jnp.where(outer, pltpu.roll(packed, 4, 0), 0.0)

    def inner_sum(slot, scale, totals):
        total0, total1 = totals
        for k in range(1, TERMS):
            for side in range(2):
                at = (k - 1) * 2 + side
                index = ti[at, slot] * TERMS + k
                weight = tf[at, slot] * scale
                total0 = total0 + weight * ak[index, 0]
                total1 = total1 + weight * ak[index, 1]
        return total0, total1

    def edge_sum(slot, first, scale, edges, faces, packed):
        for k in range(1, TERMS):
            at = first + (k - 1) * 2
            along = (tf[at, slot] * scale) * edges[ti[at, slot]] + (tf[at + 1, slot] * scale) * edges[ti[at + 1, slot]]
            packed = faces[k] * along if packed is None else packed + faces[k] * along
        return packed

    def item_copy(j):
        target = rb.at[j, pl.ds(0, 2)] if j < LATE else rl.at[j - LATE, pl.ds(0, 2)]
        return pltpu.make_async_remote_copy(
            sb.at[j], target, item_s.at[j], item_r.at[j], device_id=partner, device_id_type=MESH
        )

    def item_of(j):
        slot = ti[13, j]
        return slot, ti[14, slot], jnp.where(slot // CHIP == high, 1.0, 0.0).astype(f32)

    def slot_at(b):
        return high * CHIP + jnp.where(b < GROUP, core * GROUP + b, (1 - core) * GROUP + b - GROUP)

    def begin_item(j, carry):
        slot, place, ours = item_of(j)
        sb[j, 0], sb[j, 1] = inner_sum(slot, 1.0 - ours, (ours * m[place, 0], ours * m[place, 1]))
        return carry

    def early_item(j):
        slot, place, ours = item_of(j)
        totals = [ours * m[place, 0], ours * m[place, 1]]
        for k in range(1, TERMS):
            at = (k - 1) * 2
            weights = [tf[at + side, slot] * (1.0 - ours) for side in range(2)]
            places = [ti[at + side, slot] for side in range(2)]
            mixed = [weights[0] * m[places[0], p] + weights[1] * m[places[1], p] for p in range(3)]
            def store(_, p, value):
                totals[p] = totals[p] + value
            stencil(mixed, (k,), store)
        sb[j, 0], sb[j, 1] = totals

    for j in range(EARLY):
        early_item(j)
        item_copy(j).start()

    lax.fori_loop(0, CHIP, own_stencil, 0)
    lax.fori_loop(EARLY, EVENS, begin_item, 0)

    for there, side in downs:
        @pl.when(there)
        def _():
            for source in range(2):
                edge_copy(side, 0, source).wait_recv()

    def tile(top0, top1, bottom0, bottom1):
        return jnp.where(row == 0, top0, jnp.where(row == 7, bottom0, jnp.where(row == 4, top1, bottom1)))

    def own_edges(v0, v1):
        return jnp.where(outer, v0, pltpu.roll(v1, 4, 0))

    def arrived(ref, lead, r):
        return [ref[(side,) + lead + (pl.ds(r + p, 1), slice(None))] for side in range(2) for p in range(2)]

    left_out = jnp.logical_or(
        jnp.logical_and(low_seam, upper), jnp.logical_and(high_seam, jnp.logical_or(row == 7, row == 3))
    )
    for k in range(TERMS):
        faces = own_edges(c[k, 0], c[k, 1]) + tile(*arrived(er, (k // 2,), 10 + (k % 2) * 2))
        gh[k] = jnp.where(left_out, 0.0, 0.5 * faces)
    for b in range(CHIP):
        source = core if b < GROUP else 1 - core
        dh[b] = own_edges(m[b, 0], m[b, 1]) - tile(*arrived(er, (source,), (b % GROUP) * 2))

    tile_copy = pltpu.make_async_remote_copy(ts, tr, tile_s, tile_r, device_id=partner, device_id_type=MESH)

    for j in range(EARLY, EVENS):
        slot, place, ours = item_of(j)
        edge0, edge1 = spread(edge_sum(slot, 0, 1.0 - ours, dh, gh, None))
        sb[j, 0] = sb[j, 0] + edge0
        sb[j, 1] = sb[j, 1] + edge1
        item_copy(j).start()
        if j == LATE - 1:
            pair = []
            for n in range(EARLY):
                slot, _, ours = item_of(n)
                _, place, late_ours = item_of(LATE + n)
                pair.append(edge_sum(slot, 0, 1.0 - ours, dh, gh, late_ours * dh[place]))
            moved = jnp.where(jnp.logical_or(row == 1, row == 5), pltpu.roll(pair[1], 1, 0), pltpu.roll(pair[1], 7, 0))
            ts[...] = jnp.where(jnp.logical_or(outer, middle), pair[0], moved)
            tile_copy.start()

    def give(n, source, target):
        return pltpu.make_async_remote_copy(
            source, target, give_s.at[n], give_r.at[n], device_id=sibling, device_id_type=MESH
        )

    faces_copy = give(0, gh, ghf)
    tile_on = give(1, tr, trf)
    sums_copy = give(2, acc.at[pl.ds(GROUP, GROUP)], far)
    faces_copy.start()
    lax.fori_loop(0, TERMS, far_faces, 0)

    def local_sum(b, carry):
        slot = slot_at(b)
        weight = tf[13, slot]
        total0, total1 = inner_sum(slot, 1.0, (weight * ak[b * TERMS, 0], weight * ak[b * TERMS, 1]))
        edge0, edge1 = spread(edge_sum(slot, 0, 1.0, dh, gh, gh[0] * (weight * dh[b])))
        acc[b, 0], acc[b, 1] = total0 + edge0, total1 + edge1
        return carry

    lax.fori_loop(0, CHIP, local_sum, 0)

    def plane_copy(j):
        held, at = (rb, j) if j < LATE else (rl, j - LATE)
        return pltpu.make_async_remote_copy(
            held.at[at, pl.ds(1, 1)], held.at[at, pl.ds(2, 1)], plane_s.at[j], plane_r.at[j],
            device_id=sibling, device_id_type=MESH,
        )

    def outer_copy(n):
        return pltpu.make_async_remote_copy(
            rl.at[n, pl.ds(0, 1)], rl.at[n, pl.ds(3, 1)], outer_s.at[n], outer_r.at[n],
            device_id=sibling, device_id_type=MESH,
        )

    def edge_on(side, g):
        return pltpu.make_async_remote_copy(
            hs.at[side, g], hr.at[side, g], fwd_s.at[side, g], fwd_r.at[side, g],
            device_id=(mode, space + (1 if side == 0 else -1)), device_id_type=MESH,
        )

    def raw_stencil(j, carry):
        def store(k, p, value):
            akr[j * 3 + k - 1, p] = value
        stencil((rb[j, 0], rb[j, 1], rb[j, 2]), range(1, TERMS), store)
        return carry

    for g, members in enumerate(groups):
        for n, j in enumerate(members):
            item_copy(j).wait_recv()
            plane_copy(j).start()
            for side, r in ((0, 7), (1, 0)):
                for p in range(2):
                    hs[side, g, pl.ds(n * 2 + p, 1), :] = rb[j, p, pl.ds(r, 1), :]
        for there, side in ups:
            @pl.when(there)
            def _():
                edge_on(side, g).start()
        for j in members:
            plane_copy(j).wait_recv()
        lax.fori_loop(members[0], members[-1] + 1, raw_stencil, 0)
    def remote_sum(b, carry):
        slot = slot_at(b)
        index = ti[12, slot]
        soon = index < LATE
        weight = jnp.where(soon, tf[12, slot], 0.0)
        at = jnp.minimum(index, LATE - 1)
        total0, total1 = acc[b, 0] + weight * rb[at, 0], acc[b, 1] + weight * rb[at, 1]
        for cell in range(6):
            at = ti[6 + cell, slot]
            weight = jnp.where(at < LATE, tf[6 + cell, slot], 0.0)
            at = jnp.minimum(at, LATE - 1) * 3 + cell // 2
            total0 = total0 + weight * akr[at, 0]
            total1 = total1 + weight * akr[at, 1]
        acc[b, 0], acc[b, 1] = total0, total1
        return carry

    lax.fori_loop(0, CHIP, remote_sum, 0)

    def unpack(ref, target):
        target[0] = ref[...]
        target[1] = jnp.where(upper, pltpu.roll(ref[...], 7, 0), pltpu.roll(ref[...], 1, 0))

    tile_copy.wait_recv()
    tile_on.start()
    unpack(tr, drl)

    for g, members in enumerate(groups):
        for there, side in downs:
            @pl.when(there)
            def _():
                edge_on(side, g).wait_recv()
        for n, j in enumerate(members):
            dr[j] = own_edges(rb[j, 0], rb[j, 1]) - tile(*arrived(hr, (g,), n * 2))

    def remote_edges(b, carry):
        slot = slot_at(b)
        packed = None
        for k in range(1, TERMS):
            along = None
            for side in range(2):
                cell = 6 + (k - 1) * 2 + side
                at = ti[cell, slot]
                part = jnp.where(at < LATE, tf[cell, slot], 0.0) * dr[jnp.minimum(at, LATE - 1)]
                along = part if along is None else along + part
            packed = gh[k] * along if packed is None else packed + gh[k] * along
        edge0, edge1 = spread(packed)
        acc[b, 0] = acc[b, 0] + edge0
        acc[b, 1] = acc[b, 1] + edge1
        return carry

    lax.fori_loop(0, CHIP, remote_edges, 0)

    @pl.when(jnp.logical_not(seam))
    def _():
        sums_copy.start()

    for n in range(ENDS):
        item_copy(LATE + n).wait_recv()
        plane_copy(LATE + n).start()
        outer_copy(n).start()

    @pl.when(seam)
    def _():
        for source in range(4):
            seam_copy(0, 0, source).wait_recv()

        @pl.when(low_seam)
        def _():
            for chip in range(2):
                for other in range(2):
                    seam_copy(chip, other, mode).start()

        for source in range(2):
            pair_copy(0, source).wait_recv()

        def rows(ref, lead, r):
            return jnp.where(outer, ref[lead, pl.ds(r, 1), :], ref[lead, pl.ds(r + 1, 1), :])

        facing = jnp.logical_or(
            jnp.logical_and(low_seam, upper), jnp.logical_and(high_seam, jnp.logical_or(row == 7, row == 3))
        )
        for k in range(TERMS):
            faces = own_edges(c[k, 0], c[k, 1]) + rows(sh, high * 2 + k // 2, 10 + (k % 2) * 2)
            gs[k] = jnp.where(facing, 0.5 * faces, 0.0)
        for b in range(CHIP):
            source = high * 2 + (core if b < GROUP else 1 - core)
            ds[b] = own_edges(m[b, 0], m[b, 1]) - rows(sh, source, (b % GROUP) * 2)
            ds[CHIP + b] = rows(se, b // GROUP, (b % GROUP) * 2) - rows(sh, (1 - high) * 2 + b // GROUP, (b % GROUP) * 2)

        def seam_sum(b, carry):
            slot = slot_at(b)
            edge0, edge1 = spread(edge_sum(slot, 16, 1.0, ds, gs, gs[0] * (tf[13, slot] * ds[b])))
            acc[b, 0] = acc[b, 0] + edge0
            acc[b, 1] = acc[b, 1] + edge1
            return carry

        lax.fori_loop(0, CHIP, seam_sum, 0)
        sums_copy.start()

    def late_stencil(far_side, n):
        def store(k, p, value):
            akl[n * 3 + k - 1, p] = value
        near, mid, beyond = (3, 2, 1) if far_side else (0, 1, 2)
        stencil((rl[n, near], rl[n, mid], rl[n, beyond]), range(1, TERMS), store, far_side)

    for n in range(ENDS):
        plane_copy(LATE + n).wait_recv()
        late_stencil(False, n)
        outer_copy(n).wait_recv()
        late_stencil(True, n)
    faces_copy.wait_recv()
    tile_on.wait_recv()
    unpack(trf, drf)
    sums_copy.wait_recv()

    def late_sum(b, carry):
        slot = slot_at(b)
        index = ti[12, slot]
        late = index >= LATE
        weight = jnp.where(late, tf[12, slot], 0.0)
        at = jnp.maximum(index - LATE, 0)
        totals = [acc[b, 0], acc[b, 1], far[b, 1], far[b, 0]]
        totals = [total + weight * rl[at, p] for p, total in enumerate(totals)]
        near_edge, far_edge = 0.0, 0.0
        for n in range(ENDS):
            weight = jnp.where(index == n, tf[12, slot], 0.0)
            near_edge, far_edge = near_edge + weight * drl[n], far_edge + weight * drf[n]
            weight, term = jnp.float32(0.0), jnp.int32(0)
            for cell in range(6):
                found = ti[6 + cell, slot] == LATE + n
                weight = jnp.where(found, tf[6 + cell, slot], weight)
                term = jnp.where(found, cell // 2, term)
            totals = [total + weight * akl[n * 3 + term, p] for p, total in enumerate(totals)]
            near_edge = near_edge + gh[term + 1] * (weight * drl[n])
            far_edge = far_edge + ghf[term + 1] * (weight * drf[n])
        edges = spread(near_edge) + spread(far_edge)[::-1]
        for p in range(4):
            out[b, planes[p]] = totals[p] + edges[p]
        return carry

    lax.fori_loop(0, GROUP, late_sum, 0)

    for copy in to_sibling:
        copy.wait_send()
    for there, side in ups:
        @pl.when(there)
        def _():
            for other in range(2):
                edge_copy(side, other, core).wait_send()
            for g in range(len(groups)):
                edge_on(side, g).wait_send()

    @pl.when(seam)
    def _():
        for other in range(2):
            pair_copy(other, core).wait_send()
            for chip in range(2):
                seam_copy(chip, other, mode).wait_send()

    for j in range(EVENS):
        item_copy(j).wait_send()
        plane_copy(j).wait_send()
    for n in range(ENDS):
        outer_copy(n).wait_send()
    for copy in (tile_copy, faces_copy, tile_on, sums_copy):
        copy.wait_send()


def galerkin(spaces, modes, coefs, coupling, values, assignment):
    width = modes.shape[3]
    f32 = jnp.float32
    groups = -(-LATE // 4)
    dma = pltpu.SemaphoreType.DMA
    vmem = pltpu.VMEM
    scratch = [
        vmem((CHIP, 4, 8, width), f32),
        vmem((TERMS, 4, 8, width), f32),
        vmem((2, 2, 16, width), f32),
        vmem((2, 2, 16, width), f32),
        vmem((TERMS, 4, 8, width), f32),
        vmem((TERMS, 4, 8, width), f32),
        vmem((TERMS, 4, 8, width), f32),
        vmem((TERMS, 4, 8, width), f32),
        vmem((TERMS, 8, width), f32),
        vmem((CHIP * TERMS, 2, 8, width), f32),
        vmem((CHIP, 8, width), f32),
        vmem((EVENS, 2, 8, width), f32),
        vmem((LATE, 3, 8, width), f32),
        vmem((8, width), f32),
        vmem((8, width), f32),
        vmem((2, groups, 8, width), f32),
        vmem((2, groups, 8, width), f32),
        vmem((LATE, 8, width), f32),
        vmem((LATE * 3, 2, 8, width), f32),
        vmem((CHIP, 2, 8, width), f32),
        vmem((4, 16, width), f32),
        vmem((2, 16, width), f32),
        vmem((SLOTS, 8, width), f32),
        vmem((TERMS, 8, width), f32),
        vmem((ENDS, 4, 8, width), f32),
        vmem((ENDS * 3, 4, 8, width), f32),
        vmem((ENDS, 8, width), f32),
        vmem((TERMS, 8, width), f32),
        vmem((8, width), f32),
        vmem((ENDS, 8, width), f32),
        vmem((GROUP, 2, 8, width), f32),
        vmem(coupling.shape, jnp.int32),
        vmem(values.shape, f32),
        vmem(assignment.shape, jnp.int32),
        vmem((24, 128), jnp.int32),
        vmem((24, 128), f32),
        pltpu.SMEM((24, 128), jnp.int32),
        pltpu.SMEM((24, 128), f32),
        dma((2, 4)), dma((3,)), dma((2,)), dma((3,)), dma((3,)), dma((2, 2)), dma((2, 2)), dma((EVENS,)), dma((EVENS,)),
        dma(()), dma(()), dma((EVENS,)), dma((EVENS,)),
        dma((2, groups)), dma((2, groups)), dma((2, 2)), dma((4,)), dma((2,)), dma((2,)), dma((ENDS,)), dma((ENDS,)),
        dma((3,)), dma((3,)),
    ]
    anywhere = pl.BlockSpec(memory_space=pltpu.HBM)
    return pl.pallas_call(
        functools.partial(kernel, spaces),
        out_shape=jax.ShapeDtypeStruct(modes.shape, f32),
        in_specs=[anywhere] * 5,
        out_specs=pl.BlockSpec(memory_space=pltpu.VMEM),
        scratch_shapes=scratch,
        compiler_params=pltpu.CompilerParams(
            collective_id=0, has_side_effects=True, vmem_limit_bytes=32 * 1024 * 1024
        ),
        name="galerkin",
    )(modes, coefs, coupling, values, assignment)


def solution(mesh):
    spaces = mesh.shape["space"]

    def shards(modes, coefficients, coupling, coupling_values, assignment):
        held = [
            pltpu.with_memory_space_constraint(x, pltpu.HBM)
            for x in (modes, coefficients, coupling.T, coupling_values[None], assignment[None])
        ]
        return galerkin(spaces, *held)

    in_specs = (P("mode", None, "space", None), P(None, None, "space", None), P(), P(), P())
    out_specs = P("mode", None, "space", None)
    return jax.shard_map(shards, mesh=mesh, in_specs=in_specs, out_specs=out_specs, check_vma=False)
```

```python
import functools

import jax
import jax.numpy as jnp
from jax import lax
from jax.experimental import pallas as pl
from jax.experimental.pallas import tpu as pltpu
from jax.sharding import PartitionSpec as P

MESH = pl.DeviceIdType.MESH
EVENS = 7
SLOTS = 20
GROUP = 5
CHIP = 10
TERMS = 4
ENTRIES = 80
EARLY = 2
LATE = EVENS - 2
ENDS = EVENS - LATE
INF = 1 << 24


def tables(high, core, coupling, values, assignment):
    i32 = jnp.int32
    slot = lax.broadcasted_iota(i32, (1, SLOTS), 1)
    lane = lax.broadcasted_iota(i32, (SLOTS, SLOTS), 1)
    sub = lax.broadcasted_iota(i32, (SLOTS, SLOTS), 0)
    eye = lax.broadcasted_iota(i32, (ENTRIES, ENTRIES), 0) == lax.broadcasted_iota(i32, (ENTRIES, ENTRIES), 1)
    first, second, term = [jnp.sum(jnp.where(eye, coupling[n : n + 1], 0), axis=1, keepdims=True) for n in range(3)]
    value = jnp.sum(jnp.where(eye, values, 0.0), axis=1, keepdims=True)
    hit_first = first == assignment
    hit_second = second == assignment
    joined = jnp.logical_and(hit_first, term > 0)
    degree = jnp.sum(jnp.where(joined, 1, 0), axis=0, keepdims=True)
    five = jnp.where(degree == 5, 1, 0)
    by_five = jnp.sum(jnp.where(hit_second, five, 0), axis=1, keepdims=True)
    near_five = jnp.sum(jnp.where(joined, by_five, 0), axis=0, keepdims=True)
    even = jnp.where(jnp.logical_or(degree <= 2, near_five > 0), 0, 1)
    even_col = jnp.sum(jnp.where(lane == sub, even, 0), axis=1, keepdims=True)
    ahead = jnp.sum(jnp.where(sub < lane, even_col, 0), axis=0, keepdims=True)
    low = jnp.sum(jnp.where(sub < CHIP, even_col, 0), axis=0, keepdims=True)
    order0 = ahead
    order1 = jnp.where(slot < CHIP, ahead + (EVENS - low), ahead - low)
    mine = jnp.where(high == 0, order0, order1)
    theirs = jnp.where(high == 0, order1, order0)
    key_row = jnp.where(even > 0, mine, 99)
    key_col = jnp.sum(jnp.where(lane == sub, key_row, 0), axis=1, keepdims=True)
    slot_of = jnp.sum(jnp.where(key_col == lane, sub, 0), axis=0, keepdims=True)
    local = slot - high * CHIP
    here = jnp.logical_and(local >= 0, local < CHIP)
    place = jnp.where(core == 0, local, jnp.where(local < GROUP, local + GROUP, local - GROUP))
    place = jnp.where(here, place, CHIP + slot - (1 - high) * CHIP)
    code = slot * 8192 + theirs * 512 + place * 16 + even * 2 + jnp.where(here, 1, 0)
    code_of = jnp.sum(jnp.where(hit_second, code, 0), axis=1, keepdims=True)
    l_index, l_weight, r_index, r_weight, a_index, a_weight = [], [], [], [], [], []
    for k in range(1, TERMS):
        chosen = jnp.logical_and(hit_first, term == k)
        lower = jnp.min(jnp.where(chosen, code_of, INF), axis=0, keepdims=True)
        upper = jnp.max(jnp.where(chosen, code_of, -1), axis=0, keepdims=True)
        upper = jnp.where(upper == lower, -1, upper)
        for found, there in ((lower, lower < INF), (upper, upper >= 0)):
            weight = jnp.sum(jnp.where(jnp.logical_and(chosen, code_of == found), value, 0.0), axis=0, keepdims=True)
            is_here = (found % 2) == 1
            is_even = ((found // 2) % 2) == 1
            use_l = jnp.logical_and(there, is_here)
            use_r = jnp.logical_and(there, jnp.logical_and(is_even, jnp.logical_not(is_here)))
            l_index.append(jnp.where(use_l, (found // 16) % 32, 0))
            l_weight.append(jnp.where(use_l, weight, 0.0))
            r_index.append(jnp.where(use_r, (found // 512) % 16, 0))
            r_weight.append(jnp.where(use_r, weight, 0.0))
            a_index.append(jnp.where(there, (found // 16) % 32, 0))
            a_weight.append(jnp.where(there, weight, 0.0))
    diagonal = jnp.sum(jnp.where(jnp.logical_and(hit_first, term == 0), value, 0.0), axis=0, keepdims=True)
    zero_i = jnp.zeros_like(slot)
    zero_f = jnp.zeros_like(diagonal)
    theirs = jnp.where(even > 0, theirs, 0)
    place = jnp.where(here, place, 0)

    def within(rows, size):
        return [jnp.clip(x, 0, size - 1) for x in rows]

    l_index, r_index, a_index = within(l_index, CHIP), within(r_index, EVENS), within(a_index, SLOTS)
    ints = within([theirs], EVENS) + within([slot_of], SLOTS) + within([place], CHIP) + [zero_i]
    floats = [jnp.where(even > 0, 1.0, 0.0), diagonal, zero_f, zero_f]
    ints = jnp.concatenate(l_index + r_index + ints + a_index + [zero_i, zero_i], axis=0)
    floats = jnp.concatenate(l_weight + r_weight + floats + a_weight + [zero_f, zero_f], axis=0)
    return ints, floats


def kernel(
    spaces,
    modes, coefs, coupling, values, assignment, out,
    m, c, es, er, gy, gx, gz, db, gh, ak, dh, sb, rb, ts, tr, hs, hr, dr, akr, acc, sh, se, ds, gs,
    rl, akl, drl, ghf, trf, drf, far,
    cv, vv, av, tiv, tfv, ti, tf,
    load_sem, small_sem, table_sem, sib_s, sib_r, edge_s, edge_r, item_s, item_r, tile_s, tile_r, plane_s, plane_r,
    fwd_s, fwd_r, seam_s, seam_r, pair_s, pair_r, outer_s, outer_r, give_s, give_r, ready,
):
    f32, i32 = jnp.float32, jnp.int32
    mode, space = lax.axis_index("mode"), lax.axis_index("space")
    high, core = mode // 2, mode % 2
    half = spaces // 2
    low_seam, high_seam = space == half, space == half - 1
    seam = jnp.logical_or(low_seam, high_seam)
    has_low = jnp.logical_and(space > 0, jnp.logical_not(low_seam))
    has_high = jnp.logical_and(space < spaces - 1, jnp.logical_not(high_seam))
    seams = ((high_seam, 0, 1), (low_seam, 1, -1))
    sibling_mode = high * 2 + (1 - core)
    sibling = (sibling_mode, space)
    partner = ((1 - high) * 2 + core, space)
    diagonal = ((1 - high) * 2 + (1 - core), space)
    facing = (mode, sibling_mode, partner[0], diagonal[0])
    width = modes.shape[3]
    groups = [list(range(LATE))[i : i + 4] for i in range(0, LATE, 4)]
    planes = (3 * core, 1 + core, 2 - core, 3 - 3 * core)
    theirs = (3 - 3 * core, 2 - core, 1 + core)
    ups = ((has_high, 0), (has_low, 1))
    downs = ((has_low, 0), (has_high, 1))

    def signal(target):
        pl.semaphore_signal(barrier, inc=1, device_id=target, device_id_type=MESH)

    barrier = pltpu.get_barrier_semaphore()
    signal(sibling)
    signal(partner)
    for there, step in ((has_low, -1), (has_high, 1)):
        @pl.when(there)
        def _():
            for who in (mode, sibling_mode):
                signal((who, space + step))

    @pl.when(seam)
    def _():
        signal(diagonal)

    @pl.when(low_seam)
    def _():
        for who in facing:
            signal((who, space - 1))

    loads = []
    for at, plane in enumerate(planes):
        loads.append(pltpu.make_async_copy(modes.at[:, pl.ds(plane, 1)], m.at[pl.ds(0, GROUP), pl.ds(at, 1)], load_sem.at[0, at]))
        loads.append(pltpu.make_async_copy(coefs.at[:, pl.ds(plane, 1)], c.at[:, pl.ds(at, 1)], load_sem.at[1, at]))
    smalls = [
        pltpu.make_async_copy(source, target, small_sem.at[n])
        for n, (source, target) in enumerate(((coupling, cv), (values, vv), (assignment, av)))
    ]
    for copy in smalls + loads:
        copy.start()

    peers = 2 + 2 * has_low.astype(i32) + 2 * has_high.astype(i32) + seam.astype(i32) + 4 * high_seam.astype(i32)
    pl.semaphore_wait(barrier, peers)

    to_sibling = [
        pltpu.make_async_remote_copy(
            modes.at[:, pl.ds(plane, 1)], m.at[pl.ds(GROUP, GROUP), pl.ds(at, 1)],
            sib_s.at[at], sib_r.at[at], device_id=sibling, device_id_type=MESH,
        )
        for at, plane in enumerate(theirs)
    ]
    for copy in to_sibling:
        copy.start()

    for copy in smalls:
        copy.wait()
    tiv[...] = jnp.zeros(tiv.shape, i32)
    tfv[...] = jnp.zeros(tfv.shape, f32)
    tiv[:, 0:SLOTS], tfv[:, 0:SLOTS] = tables(high, core, cv[...], vv[...], av[...])
    table_copies = [
        pltpu.make_async_copy(tiv, ti, table_sem.at[0]),
        pltpu.make_async_copy(tfv, tf, table_sem.at[1]),
    ]
    for copy in table_copies:
        copy.start()

    for copy in loads:
        copy.wait()

    for side, row in ((0, 7), (1, 0)):
        for other, held in ((0, (0, 1)), (1, (3, 2))):
            for p in range(2):
                for i in range(GROUP):
                    es[side, other, pl.ds(i * 2 + p, 1), :] = m[i, held[p], pl.ds(row, 1), :]
                for kk in range(2):
                    es[side, other, pl.ds(10 + kk * 2 + p, 1), :] = c[2 * core + kk, held[p], pl.ds(row, 1), :]

    def edge_copy(side, other, source):
        who = mode if other == 0 else sibling_mode
        return pltpu.make_async_remote_copy(
            es.at[side, other], er.at[side, source], edge_s.at[side, other], edge_r.at[side, source],
            device_id=(who, space + (1 if side == 0 else -1)), device_id_type=MESH,
        )

    def seam_copy(side, step, n, source):
        return pltpu.make_async_remote_copy(
            es.at[side, n % 2], sh.at[source], seam_s.at[n], seam_r.at[source],
            device_id=(facing[n], space + step), device_id_type=MESH,
        )

    def pair_copy(side, other, source):
        return pltpu.make_async_remote_copy(
            es.at[side, other], se.at[source], pair_s.at[other], pair_r.at[source],
            device_id=partner if other == 0 else diagonal, device_id_type=MESH,
        )

    @pl.when(high_seam)
    def _():
        for who in facing:
            pl.semaphore_signal(ready, inc=1, device_id=(who, space + 1), device_id_type=MESH)
        for n in range(4):
            seam_copy(0, 1, n, mode).start()

    for there, side in ups:
        @pl.when(there)
        def _():
            for other in range(2):
                edge_copy(side, other, core).start()

    for there, side, _ in seams:
        @pl.when(there)
        def _():
            for other in range(2):
                pair_copy(side, other, core).start()

    for there, side in downs:
        @pl.when(jnp.logical_not(there))
        def _():
            er[side] = jnp.zeros(er.shape[1:], f32)
            hr[side] = jnp.zeros(hr.shape[1:], f32)

    row = lax.broadcasted_iota(i32, (8, width), 0)
    col = lax.broadcasted_iota(i32, (8, width), 1)

    def along_plane(k, p, carry):
        a = 0.5 * c[k, p]
        gy[k, p] = jnp.where(col == 0, 0.0, a + pltpu.roll(a, 1, 1))
        gx[k, p] = jnp.where(row == 0, 0.0, a + pltpu.roll(a, 1, 0))
        side = jnp.where(jnp.logical_or(col == 0, col == width - 1), 1.0, 0.0)
        db[k, p] = a * (side + carry)

    def near_faces(k, carry):
        along_plane(k, 0, 1.0)
        along_plane(k, 1, 0.0)
        gz[k, 0] = 0.5 * (c[k, 0] + c[k, 1])
        gz[k, 1] = 0.5 * (c[k, 1] + c[k, 2])
        return carry

    def far_faces(k, carry):
        along_plane(k, 3, 1.0)
        along_plane(k, 2, 0.0)
        gz[k, 2] = 0.5 * (c[k, 2] + c[k, 3])
        return carry

    def stencil(v, terms, store, far_side=False):
        p0, p1, z0 = (3, 2, 2) if far_side else (0, 1, 0)
        v0, v1, vh = v
        d0, d1 = v0 - v1, v1 - vh
        y0, y1 = v0 - pltpu.roll(v0, 1, 1), v1 - pltpu.roll(v1, 1, 1)
        x0, x1 = v0 - pltpu.roll(v0, 1, 0), v1 - pltpu.roll(v1, 1, 0)
        for k in terms:
            between = gz[k, z0] * d0
            f = gy[k, p0] * y0
            g = gx[k, p0] * x0
            store(k, p0, (f - pltpu.roll(f, width - 1, 1)) + (g - pltpu.roll(g, 7, 0)) + (between + db[k, p0] * v0))
            f = gy[k, p1] * y1
            g = gx[k, p1] * x1
            store(k, p1, (f - pltpu.roll(f, width - 1, 1)) + (g - pltpu.roll(g, 7, 0)) + (gz[k, 1] * d1 + db[k, p1] * v1 - between))

    def own_stencil(b, carry):
        def store(k, p, value):
            ak[b * TERMS + k, p] = value
        stencil((m[b, 0], m[b, 1], m[b, 2]), range(TERMS), store)
        return carry

    lax.fori_loop(0, TERMS, near_faces, 0)
    for copy in table_copies:
        copy.wait()
    for copy in to_sibling:
        copy.wait_recv()

    outer = jnp.logical_or(row == 0, row == 7)
    middle = jnp.logical_or(row == 3, row == 4)
    upper = jnp.logical_or(row == 0, row == 4)

    def spread(packed):
        return jnp.where(outer, packed, 0.0), jnp.where(outer, pltpu.roll(packed, 4, 0), 0.0)

    def inner_sum(slot, scale, totals):
        total0, total1 = totals
        for k in range(1, TERMS):
            for side in range(2):
                at = (k - 1) * 2 + side
                index = ti[at, slot] * TERMS + k
                weight = tf[at, slot] * scale
                total0 = total0 + weight * ak[index, 0]
                total1 = total1 + weight * ak[index, 1]
        return total0, total1

    def edge_sum(slot, first, scale, edges, faces, packed):
        for k in range(1, TERMS):
            at = first + (k - 1) * 2
            along = (tf[at, slot] * scale) * edges[ti[at, slot]] + (tf[at + 1, slot] * scale) * edges[ti[at + 1, slot]]
            packed = faces[k] * along if packed is None else packed + faces[k] * along
        return packed

    def item_copy(j):
        target = rb.at[j, pl.ds(0, 2)] if j < LATE else rl.at[j - LATE, pl.ds(0, 2)]
        return pltpu.make_async_remote_copy(
            sb.at[j], target, item_s.at[j], item_r.at[j], device_id=partner, device_id_type=MESH
        )

    def item_of(j):
        slot = ti[13, j]
        return slot, ti[14, slot], jnp.where(slot // CHIP == high, 1.0, 0.0).astype(f32)

    def slot_at(b):
        return high * CHIP + jnp.where(b < GROUP, core * GROUP + b, (1 - core) * GROUP + b - GROUP)

    def begin_item(j, carry):
        slot, place, ours = item_of(j)
        sb[j, 0], sb[j, 1] = inner_sum(slot, 1.0 - ours, (ours * m[place, 0], ours * m[place, 1]))
        return carry

    def early_item(j):
        slot, place, ours = item_of(j)
        totals = [ours * m[place, 0], ours * m[place, 1]]
        for k in range(1, TERMS):
            at = (k - 1) * 2
            weights = [tf[at + side, slot] * (1.0 - ours) for side in range(2)]
            places = [ti[at + side, slot] for side in range(2)]
            mixed = [weights[0] * m[places[0], p] + weights[1] * m[places[1], p] for p in range(3)]
            def store(_, p, value):
                totals[p] = totals[p] + value
            stencil(mixed, (k,), store)
        sb[j, 0], sb[j, 1] = totals

    for j in range(EARLY):
        early_item(j)
        item_copy(j).start()

    lax.fori_loop(0, CHIP, own_stencil, 0)
    lax.fori_loop(EARLY, EVENS, begin_item, 0)

    for there, side in downs:
        @pl.when(there)
        def _():
            for source in range(2):
                edge_copy(side, 0, source).wait_recv()

    def tile(top0, top1, bottom0, bottom1):
        return jnp.where(row == 0, top0, jnp.where(row == 7, bottom0, jnp.where(row == 4, top1, bottom1)))

    def own_edges(v0, v1):
        return jnp.where(outer, v0, pltpu.roll(v1, 4, 0))

    def arrived(ref, lead, r):
        return [ref[(side,) + lead + (pl.ds(r + p, 1), slice(None))] for side in range(2) for p in range(2)]

    left_out = jnp.logical_or(
        jnp.logical_and(low_seam, upper), jnp.logical_and(high_seam, jnp.logical_or(row == 7, row == 3))
    )
    for k in range(TERMS):
        faces = own_edges(c[k, 0], c[k, 1]) + tile(*arrived(er, (k // 2,), 10 + (k % 2) * 2))
        gh[k] = jnp.where(left_out, 0.0, 0.5 * faces)
    for b in range(CHIP):
        source = core if b < GROUP else 1 - core
        dh[b] = own_edges(m[b, 0], m[b, 1]) - tile(*arrived(er, (source,), (b % GROUP) * 2))

    tile_copy = pltpu.make_async_remote_copy(ts, tr, tile_s, tile_r, device_id=partner, device_id_type=MESH)

    for j in range(EARLY, EVENS):
        slot, place, ours = item_of(j)
        edge0, edge1 = spread(edge_sum(slot, 0, 1.0 - ours, dh, gh, None))
        sb[j, 0] = sb[j, 0] + edge0
        sb[j, 1] = sb[j, 1] + edge1
        item_copy(j).start()
        if j == LATE - 1:
            pair = []
            for n in range(EARLY):
                slot, _, ours = item_of(n)
                _, place, late_ours = item_of(LATE + n)
                pair.append(edge_sum(slot, 0, 1.0 - ours, dh, gh, late_ours * dh[place]))
            moved = jnp.where(jnp.logical_or(row == 1, row == 5), pltpu.roll(pair[1], 1, 0), pltpu.roll(pair[1], 7, 0))
            ts[...] = jnp.where(jnp.logical_or(outer, middle), pair[0], moved)
            tile_copy.start()

    def give(n, source, target):
        return pltpu.make_async_remote_copy(
            source, target, give_s.at[n], give_r.at[n], device_id=sibling, device_id_type=MESH
        )

    faces_copy = give(0, gh, ghf)
    tile_on = give(1, tr, trf)
    sums_copy = give(2, acc.at[pl.ds(GROUP, GROUP)], far)
    faces_copy.start()
    lax.fori_loop(0, TERMS, far_faces, 0)

    def local_sum(b, carry):
        slot = slot_at(b)
        weight = tf[13, slot]
        total0, total1 = inner_sum(slot, 1.0, (weight * ak[b * TERMS, 0], weight * ak[b * TERMS, 1]))
        edge0, edge1 = spread(edge_sum(slot, 0, 1.0, dh, gh, gh[0] * (weight * dh[b])))
        acc[b, 0], acc[b, 1] = total0 + edge0, total1 + edge1
        return carry

    lax.fori_loop(0, CHIP, local_sum, 0)

    def plane_copy(j):
        held, at = (rb, j) if j < LATE else (rl, j - LATE)
        return pltpu.make_async_remote_copy(
            held.at[at, pl.ds(1, 1)], held.at[at, pl.ds(2, 1)], plane_s.at[j], plane_r.at[j],
            device_id=sibling, device_id_type=MESH,
        )

    def outer_copy(n):
        return pltpu.make_async_remote_copy(
            rl.at[n, pl.ds(0, 1)], rl.at[n, pl.ds(3, 1)], outer_s.at[n], outer_r.at[n],
            device_id=sibling, device_id_type=MESH,
        )

    def edge_on(side, g):
        return pltpu.make_async_remote_copy(
            hs.at[side, g], hr.at[side, g], fwd_s.at[side, g], fwd_r.at[side, g],
            device_id=(mode, space + (1 if side == 0 else -1)), device_id_type=MESH,
        )

    def raw_stencil(j, carry):
        def store(k, p, value):
            akr[j * 3 + k - 1, p] = value
        stencil((rb[j, 0], rb[j, 1], rb[j, 2]), range(1, TERMS), store)
        return carry

    for g, members in enumerate(groups):
        for n, j in enumerate(members):
            item_copy(j).wait_recv()
            plane_copy(j).start()
            for side, r in ((0, 7), (1, 0)):
                for p in range(2):
                    hs[side, g, pl.ds(n * 2 + p, 1), :] = rb[j, p, pl.ds(r, 1), :]
        for there, side in ups:
            @pl.when(there)
            def _():
                edge_on(side, g).start()
        for j in members:
            plane_copy(j).wait_recv()
        lax.fori_loop(members[0], members[-1] + 1, raw_stencil, 0)
    def remote_sum(b, carry):
        slot = slot_at(b)
        index = ti[12, slot]
        soon = index < LATE
        weight = jnp.where(soon, tf[12, slot], 0.0)
        at = jnp.minimum(index, LATE - 1)
        total0, total1 = acc[b, 0] + weight * rb[at, 0], acc[b, 1] + weight * rb[at, 1]
        for cell in range(6):
            at = ti[6 + cell, slot]
            weight = jnp.where(at < LATE, tf[6 + cell, slot], 0.0)
            at = jnp.minimum(at, LATE - 1) * 3 + cell // 2
            total0 = total0 + weight * akr[at, 0]
            total1 = total1 + weight * akr[at, 1]
        acc[b, 0], acc[b, 1] = total0, total1
        return carry

    lax.fori_loop(0, CHIP, remote_sum, 0)

    def unpack(ref, target):
        target[0] = ref[...]
        target[1] = jnp.where(upper, pltpu.roll(ref[...], 7, 0), pltpu.roll(ref[...], 1, 0))

    tile_copy.wait_recv()
    tile_on.start()
    unpack(tr, drl)

    for g, members in enumerate(groups):
        for there, side in downs:
            @pl.when(there)
            def _():
                edge_on(side, g).wait_recv()
        for n, j in enumerate(members):
            dr[j] = own_edges(rb[j, 0], rb[j, 1]) - tile(*arrived(hr, (g,), n * 2))

    def remote_edges(b, carry):
        slot = slot_at(b)
        packed = None
        for k in range(1, TERMS):
            along = None
            for side in range(2):
                cell = 6 + (k - 1) * 2 + side
                at = ti[cell, slot]
                part = jnp.where(at < LATE, tf[cell, slot], 0.0) * dr[jnp.minimum(at, LATE - 1)]
                along = part if along is None else along + part
            packed = gh[k] * along if packed is None else packed + gh[k] * along
        edge0, edge1 = spread(packed)
        acc[b, 0] = acc[b, 0] + edge0
        acc[b, 1] = acc[b, 1] + edge1
        return carry

    lax.fori_loop(0, CHIP, remote_edges, 0)

    @pl.when(jnp.logical_not(seam))
    def _():
        sums_copy.start()

    for n in range(ENDS):
        item_copy(LATE + n).wait_recv()
        plane_copy(LATE + n).start()
        outer_copy(n).start()

    for there, side, step in seams:
        @pl.when(there)
        def _():
            for source in range(4):
                seam_copy(side, step, 0, source).wait_recv()
            for source in range(2):
                pair_copy(side, 0, source).wait_recv()

    @pl.when(low_seam)
    def _():
        pl.semaphore_wait(ready, 4)
        for n in range(4):
            seam_copy(1, -1, n, mode).start()

    @pl.when(seam)
    def _():
        def rows(ref, lead, r):
            return jnp.where(outer, ref[lead, pl.ds(r, 1), :], ref[lead, pl.ds(r + 1, 1), :])

        beside = jnp.logical_or(
            jnp.logical_and(low_seam, upper), jnp.logical_and(high_seam, jnp.logical_or(row == 7, row == 3))
        )
        for k in range(TERMS):
            faces = own_edges(c[k, 0], c[k, 1]) + rows(sh, high * 2 + k // 2, 10 + (k % 2) * 2)
            gs[k] = jnp.where(beside, 0.5 * faces, 0.0)
        for b in range(CHIP):
            source = high * 2 + (core if b < GROUP else 1 - core)
            ds[b] = own_edges(m[b, 0], m[b, 1]) - rows(sh, source, (b % GROUP) * 2)
            ds[CHIP + b] = rows(se, b // GROUP, (b % GROUP) * 2) - rows(sh, (1 - high) * 2 + b // GROUP, (b % GROUP) * 2)

        def seam_sum(b, carry):
            slot = slot_at(b)
            edge0, edge1 = spread(edge_sum(slot, 16, 1.0, ds, gs, gs[0] * (tf[13, slot] * ds[b])))
            acc[b, 0] = acc[b, 0] + edge0
            acc[b, 1] = acc[b, 1] + edge1
            return carry

        lax.fori_loop(0, CHIP, seam_sum, 0)
        sums_copy.start()

    def late_stencil(far_side, n):
        def store(k, p, value):
            akl[n * 3 + k - 1, p] = value
        near, mid, beyond = (3, 2, 1) if far_side else (0, 1, 2)
        stencil((rl[n, near], rl[n, mid], rl[n, beyond]), range(1, TERMS), store, far_side)

    for n in range(ENDS):
        plane_copy(LATE + n).wait_recv()
        late_stencil(False, n)
        outer_copy(n).wait_recv()
        late_stencil(True, n)
    faces_copy.wait_recv()
    tile_on.wait_recv()
    unpack(trf, drf)
    sums_copy.wait_recv()

    def late_sum(b, carry):
        slot = slot_at(b)
        index = ti[12, slot]
        late = index >= LATE
        weight = jnp.where(late, tf[12, slot], 0.0)
        at = jnp.maximum(index - LATE, 0)
        totals = [acc[b, 0], acc[b, 1], far[b, 1], far[b, 0]]
        totals = [total + weight * rl[at, p] for p, total in enumerate(totals)]
        near_edge, far_edge = 0.0, 0.0
        for n in range(ENDS):
            weight = jnp.where(index == n, tf[12, slot], 0.0)
            near_edge, far_edge = near_edge + weight * drl[n], far_edge + weight * drf[n]
            weight, term = jnp.float32(0.0), jnp.int32(0)
            for cell in range(6):
                found = ti[6 + cell, slot] == LATE + n
                weight = jnp.where(found, tf[6 + cell, slot], weight)
                term = jnp.where(found, cell // 2, term)
            totals = [total + weight * akl[n * 3 + term, p] for p, total in enumerate(totals)]
            near_edge = near_edge + gh[term + 1] * (weight * drl[n])
            far_edge = far_edge + ghf[term + 1] * (weight * drf[n])
        edges = spread(near_edge) + spread(far_edge)[::-1]
        for p in range(4):
            out[b, planes[p]] = totals[p] + edges[p]
        return carry

    lax.fori_loop(0, GROUP, late_sum, 0)

    for copy in to_sibling:
        copy.wait_send()
    for there, side in ups:
        @pl.when(there)
        def _():
            for other in range(2):
                edge_copy(side, other, core).wait_send()
            for g in range(len(groups)):
                edge_on(side, g).wait_send()

    for there, side, step in seams:
        @pl.when(there)
        def _():
            for other in range(2):
                pair_copy(side, other, core).wait_send()
            for n in range(4):
                seam_copy(side, step, n, mode).wait_send()

    for j in range(EVENS):
        item_copy(j).wait_send()
        plane_copy(j).wait_send()
    for n in range(ENDS):
        outer_copy(n).wait_send()
    for copy in (tile_copy, faces_copy, tile_on, sums_copy):
        copy.wait_send()


def galerkin(spaces, modes, coefs, coupling, values, assignment):
    width = modes.shape[3]
    f32 = jnp.float32
    groups = -(-LATE // 4)
    dma = pltpu.SemaphoreType.DMA
    vmem = pltpu.VMEM
    scratch = [
        vmem((CHIP, 4, 8, width), f32),
        vmem((TERMS, 4, 8, width), f32),
        vmem((2, 2, 16, width), f32),
        vmem((2, 2, 16, width), f32),
        vmem((TERMS, 4, 8, width), f32),
        vmem((TERMS, 4, 8, width), f32),
        vmem((TERMS, 4, 8, width), f32),
        vmem((TERMS, 4, 8, width), f32),
        vmem((TERMS, 8, width), f32),
        vmem((CHIP * TERMS, 2, 8, width), f32),
        vmem((CHIP, 8, width), f32),
        vmem((EVENS, 2, 8, width), f32),
        vmem((LATE, 3, 8, width), f32),
        vmem((8, width), f32),
        vmem((8, width), f32),
        vmem((2, groups, 8, width), f32),
        vmem((2, groups, 8, width), f32),
        vmem((LATE, 8, width), f32),
        vmem((LATE * 3, 2, 8, width), f32),
        vmem((CHIP, 2, 8, width), f32),
        vmem((4, 16, width), f32),
        vmem((2, 16, width), f32),
        vmem((SLOTS, 8, width), f32),
        vmem((TERMS, 8, width), f32),
        vmem((ENDS, 4, 8, width), f32),
        vmem((ENDS * 3, 4, 8, width), f32),
        vmem((ENDS, 8, width), f32),
        vmem((TERMS, 8, width), f32),
        vmem((8, width), f32),
        vmem((ENDS, 8, width), f32),
        vmem((GROUP, 2, 8, width), f32),
        vmem(coupling.shape, jnp.int32),
        vmem(values.shape, f32),
        vmem(assignment.shape, jnp.int32),
        vmem((24, 128), jnp.int32),
        vmem((24, 128), f32),
        pltpu.SMEM((24, 128), jnp.int32),
        pltpu.SMEM((24, 128), f32),
        dma((2, 4)), dma((3,)), dma((2,)), dma((3,)), dma((3,)), dma((2, 2)), dma((2, 2)), dma((EVENS,)), dma((EVENS,)),
        dma(()), dma(()), dma((EVENS,)), dma((EVENS,)),
        dma((2, groups)), dma((2, groups)), dma((4,)), dma((4,)), dma((2,)), dma((2,)), dma((ENDS,)), dma((ENDS,)),
        dma((3,)), dma((3,)), pltpu.SemaphoreType.REGULAR,
    ]
    anywhere = pl.BlockSpec(memory_space=pltpu.HBM)
    return pl.pallas_call(
        functools.partial(kernel, spaces),
        out_shape=jax.ShapeDtypeStruct(modes.shape, f32),
        in_specs=[anywhere] * 5,
        out_specs=pl.BlockSpec(memory_space=pltpu.VMEM),
        scratch_shapes=scratch,
        compiler_params=pltpu.CompilerParams(
            collective_id=0, has_side_effects=True, vmem_limit_bytes=32 * 1024 * 1024
        ),
        name="galerkin",
    )(modes, coefs, coupling, values, assignment)


def solution(mesh):
    spaces = mesh.shape["space"]

    def shards(modes, coefficients, coupling, coupling_values, assignment):
        held = [
            pltpu.with_memory_space_constraint(x, pltpu.HBM)
            for x in (modes, coefficients, coupling.T, coupling_values[None], assignment[None])
        ]
        return galerkin(spaces, *held)

    in_specs = (P("mode", None, "space", None), P(None, None, "space", None), P(), P(), P())
    out_specs = P("mode", None, "space", None)
    return jax.shard_map(shards, mesh=mesh, in_specs=in_specs, out_specs=out_specs, check_vma=False)
```

```python
import functools

import jax
import jax.numpy as jnp
from jax import lax
from jax.experimental import pallas as pl
from jax.experimental.pallas import tpu as pltpu
from jax.sharding import PartitionSpec as P

MESH = pl.DeviceIdType.MESH
EVENS = 7
SLOTS = 20
GROUP = 5
CHIP = 10
TERMS = 4
ENTRIES = 80
EARLY = 4
LATE = EARLY
FIRST = 2
ENDS = EVENS - LATE
INF = 1 << 24


def tables(high, core, coupling, values, assignment):
    i32 = jnp.int32
    slot = lax.broadcasted_iota(i32, (1, SLOTS), 1)
    lane = lax.broadcasted_iota(i32, (SLOTS, SLOTS), 1)
    sub = lax.broadcasted_iota(i32, (SLOTS, SLOTS), 0)
    eye = lax.broadcasted_iota(i32, (ENTRIES, ENTRIES), 0) == lax.broadcasted_iota(i32, (ENTRIES, ENTRIES), 1)
    first, second, term = [jnp.sum(jnp.where(eye, coupling[n : n + 1], 0), axis=1, keepdims=True) for n in range(3)]
    value = jnp.sum(jnp.where(eye, values, 0.0), axis=1, keepdims=True)
    hit_first = first == assignment
    hit_second = second == assignment
    joined = jnp.logical_and(hit_first, term > 0)
    degree = jnp.sum(jnp.where(joined, 1, 0), axis=0, keepdims=True)
    five = jnp.where(degree == 5, 1, 0)
    by_five = jnp.sum(jnp.where(hit_second, five, 0), axis=1, keepdims=True)
    near_five = jnp.sum(jnp.where(joined, by_five, 0), axis=0, keepdims=True)
    even = jnp.where(jnp.logical_or(degree <= 2, near_five > 0), 0, 1)
    even_col = jnp.sum(jnp.where(lane == sub, even, 0), axis=1, keepdims=True)
    ahead = jnp.sum(jnp.where(sub < lane, even_col, 0), axis=0, keepdims=True)
    low = jnp.sum(jnp.where(sub < CHIP, even_col, 0), axis=0, keepdims=True)
    order0 = ahead
    order1 = jnp.where(slot < CHIP, ahead + (EVENS - low), ahead - low)
    mine = jnp.where(high == 0, order0, order1)
    theirs = jnp.where(high == 0, order1, order0)
    key_row = jnp.where(even > 0, mine, 99)
    key_col = jnp.sum(jnp.where(lane == sub, key_row, 0), axis=1, keepdims=True)
    slot_of = jnp.sum(jnp.where(key_col == lane, sub, 0), axis=0, keepdims=True)
    local = slot - high * CHIP
    here = jnp.logical_and(local >= 0, local < CHIP)
    place = jnp.where(core == 0, local, jnp.where(local < GROUP, local + GROUP, local - GROUP))
    place = jnp.where(here, place, CHIP + slot - (1 - high) * CHIP)
    code = slot * 8192 + theirs * 512 + place * 16 + even * 2 + jnp.where(here, 1, 0)
    code_of = jnp.sum(jnp.where(hit_second, code, 0), axis=1, keepdims=True)
    l_index, l_weight, r_index, r_weight, a_index, a_weight = [], [], [], [], [], []
    for k in range(1, TERMS):
        chosen = jnp.logical_and(hit_first, term == k)
        lower = jnp.min(jnp.where(chosen, code_of, INF), axis=0, keepdims=True)
        upper = jnp.max(jnp.where(chosen, code_of, -1), axis=0, keepdims=True)
        upper = jnp.where(upper == lower, -1, upper)
        for found, there in ((lower, lower < INF), (upper, upper >= 0)):
            weight = jnp.sum(jnp.where(jnp.logical_and(chosen, code_of == found), value, 0.0), axis=0, keepdims=True)
            is_here = (found % 2) == 1
            is_even = ((found // 2) % 2) == 1
            use_l = jnp.logical_and(there, is_here)
            use_r = jnp.logical_and(there, jnp.logical_and(is_even, jnp.logical_not(is_here)))
            l_index.append(jnp.where(use_l, (found // 16) % 32, 0))
            l_weight.append(jnp.where(use_l, weight, 0.0))
            r_index.append(jnp.where(use_r, (found // 512) % 16, 0))
            r_weight.append(jnp.where(use_r, weight, 0.0))
            a_index.append(jnp.where(there, (found // 16) % 32, 0))
            a_weight.append(jnp.where(there, weight, 0.0))
    diagonal = jnp.sum(jnp.where(jnp.logical_and(hit_first, term == 0), value, 0.0), axis=0, keepdims=True)
    zero_i = jnp.zeros_like(slot)
    zero_f = jnp.zeros_like(diagonal)
    theirs = jnp.where(even > 0, theirs, 0)
    place = jnp.where(here, place, 0)

    def within(rows, size):
        return [jnp.clip(x, 0, size - 1) for x in rows]

    l_index, r_index, a_index = within(l_index, CHIP), within(r_index, EVENS), within(a_index, SLOTS)
    ints = within([theirs], EVENS) + within([slot_of], SLOTS) + within([place], CHIP) + [zero_i]
    floats = [jnp.where(even > 0, 1.0, 0.0), diagonal, zero_f, zero_f]
    ints = jnp.concatenate(l_index + r_index + ints + a_index + [zero_i, zero_i], axis=0)
    floats = jnp.concatenate(l_weight + r_weight + floats + a_weight + [zero_f, zero_f], axis=0)
    return ints, floats


def kernel(
    spaces,
    modes, coefs, coupling, values, assignment, out,
    m, c, es, er, gy, gx, gz, db, gh, ak, dh, sb, rb, ts, tr, hs, hr, dr, akr, acc, sh, se, ds, gs,
    rl, akl, drl, ghf, trf, drf, far, sp, sq,
    cv, vv, av, tiv, tfv, ti, tf,
    load_sem, small_sem, table_sem, sib_s, sib_r, edge_s, edge_r, item_s, item_r, tile_s, tile_r, plane_s, plane_r,
    fwd_s, fwd_r, seam_s, seam_r, pair_s, pair_r, outer_s, outer_r, give_s, give_r, ready,
):
    f32, i32 = jnp.float32, jnp.int32
    mode, space = lax.axis_index("mode"), lax.axis_index("space")
    high, core = mode // 2, mode % 2
    half = spaces // 2
    low_seam, high_seam = space == half, space == half - 1
    seam = jnp.logical_or(low_seam, high_seam)
    has_low = jnp.logical_and(space > 0, jnp.logical_not(low_seam))
    has_high = jnp.logical_and(space < spaces - 1, jnp.logical_not(high_seam))
    seams = ((high_seam, 0, 1), (low_seam, 1, -1))
    sibling_mode = high * 2 + (1 - core)
    sibling = (sibling_mode, space)
    partner = ((1 - high) * 2 + core, space)
    diagonal = ((1 - high) * 2 + (1 - core), space)
    facing = (mode, sibling_mode, partner[0], diagonal[0])
    width = modes.shape[3]
    groups = [list(range(LATE))[i : i + 4] for i in range(0, LATE, 4)]
    planes = (3 * core, 1 + core, 2 - core, 3 - 3 * core)
    ups = ((has_high, 0), (has_low, 1))
    downs = ((has_low, 0), (has_high, 1))

    def signal(target):
        pl.semaphore_signal(barrier, inc=1, device_id=target, device_id_type=MESH)

    barrier = pltpu.get_barrier_semaphore()
    signal(sibling)
    signal(partner)
    for there, step in ((has_low, -1), (has_high, 1)):
        @pl.when(there)
        def _():
            for who in (mode, sibling_mode):
                signal((who, space + step))

    @pl.when(seam)
    def _():
        signal(diagonal)

    @pl.when(low_seam)
    def _():
        for who in facing:
            signal((who, space - 1))

    loads = []
    for at, plane in enumerate(planes):
        loads.append(pltpu.make_async_copy(modes.at[:, pl.ds(plane, 1)], m.at[pl.ds(0, GROUP), pl.ds(at, 1)], load_sem.at[0, at]))
        loads.append(pltpu.make_async_copy(coefs.at[:, pl.ds(plane, 1)], c.at[:, pl.ds(at, 1)], load_sem.at[1, at]))
    smalls = [
        pltpu.make_async_copy(source, target, small_sem.at[n])
        for n, (source, target) in enumerate(((coupling, cv), (values, vv), (assignment, av)))
    ]
    for copy in smalls + loads:
        copy.start()

    for copy in smalls:
        copy.wait()
    tiv[...] = jnp.zeros(tiv.shape, i32)
    tfv[...] = jnp.zeros(tfv.shape, f32)
    tiv[:, 0:SLOTS], tfv[:, 0:SLOTS] = tables(high, core, cv[...], vv[...], av[...])
    table_copies = [
        pltpu.make_async_copy(tiv, ti, table_sem.at[0]),
        pltpu.make_async_copy(tfv, tf, table_sem.at[1]),
    ]
    for copy in table_copies:
        copy.start()

    peers = 2 + 2 * has_low.astype(i32) + 2 * has_high.astype(i32) + seam.astype(i32) + 4 * high_seam.astype(i32)
    pl.semaphore_wait(barrier, peers)

    for copy in loads:
        copy.wait()

    to_sibling = [
        pltpu.make_async_remote_copy(
            m.at[pl.ds(0, GROUP), pl.ds(3 - at, 1)], m.at[pl.ds(GROUP, GROUP), pl.ds(at, 1)],
            sib_s.at[at], sib_r.at[at], device_id=sibling, device_id_type=MESH,
        )
        for at in range(3)
    ]
    for copy in to_sibling:
        copy.start()

    for side, row in ((0, 7), (1, 0)):
        for other, held in ((0, (0, 1)), (1, (3, 2))):
            for p in range(2):
                for i in range(GROUP):
                    es[side, other, pl.ds(i * 2 + p, 1), :] = m[i, held[p], pl.ds(row, 1), :]
                for kk in range(2):
                    es[side, other, pl.ds(10 + kk * 2 + p, 1), :] = c[2 * core + kk, held[p], pl.ds(row, 1), :]

    def edge_copy(side, other, source):
        who = mode if other == 0 else sibling_mode
        return pltpu.make_async_remote_copy(
            es.at[side, other], er.at[side, source], edge_s.at[side, other], edge_r.at[side, source],
            device_id=(who, space + (1 if side == 0 else -1)), device_id_type=MESH,
        )

    def seam_copy(side, step, n, source):
        return pltpu.make_async_remote_copy(
            es.at[side, n % 2], sh.at[source], seam_s.at[n], seam_r.at[source],
            device_id=(facing[n], space + step), device_id_type=MESH,
        )

    def pair_copy(side, other, source):
        return pltpu.make_async_remote_copy(
            es.at[side, other], se.at[source], pair_s.at[other], pair_r.at[source],
            device_id=partner if other == 0 else diagonal, device_id_type=MESH,
        )

    @pl.when(high_seam)
    def _():
        for who in facing:
            pl.semaphore_signal(ready, inc=1, device_id=(who, space + 1), device_id_type=MESH)
        for n in range(4):
            seam_copy(0, 1, n, mode).start()

    for there, side in ups:
        @pl.when(there)
        def _():
            for other in range(2):
                edge_copy(side, other, core).start()

    for there, side, _ in seams:
        @pl.when(there)
        def _():
            for other in range(2):
                pair_copy(side, other, core).start()

    for there, side in downs:
        @pl.when(jnp.logical_not(there))
        def _():
            er[side] = jnp.zeros(er.shape[1:], f32)
            hr[side] = jnp.zeros(hr.shape[1:], f32)

    row = lax.broadcasted_iota(i32, (8, width), 0)
    col = lax.broadcasted_iota(i32, (8, width), 1)

    def along_plane(k, p, carry):
        a = 0.5 * c[k, p]
        gy[k, p] = jnp.where(col == 0, 0.0, a + pltpu.roll(a, 1, 1))
        gx[k, p] = jnp.where(row == 0, 0.0, a + pltpu.roll(a, 1, 0))
        side = jnp.where(jnp.logical_or(col == 0, col == width - 1), 1.0, 0.0)
        db[k, p] = a * (side + carry)

    def near_faces(k, carry):
        along_plane(k, 0, 1.0)
        along_plane(k, 1, 0.0)
        gz[k, 0] = 0.5 * (c[k, 0] + c[k, 1])
        gz[k, 1] = 0.5 * (c[k, 1] + c[k, 2])
        return carry

    def far_faces(k, carry):
        along_plane(k, 3, 1.0)
        along_plane(k, 2, 0.0)
        gz[k, 2] = 0.5 * (c[k, 2] + c[k, 3])
        return carry

    def stencil(v, terms, store, far_side=False):
        p0, p1, z0 = (3, 2, 2) if far_side else (0, 1, 0)
        v0, v1, vh = v
        d0, d1 = v0 - v1, v1 - vh
        y0, y1 = v0 - pltpu.roll(v0, 1, 1), v1 - pltpu.roll(v1, 1, 1)
        x0, x1 = v0 - pltpu.roll(v0, 1, 0), v1 - pltpu.roll(v1, 1, 0)
        for k in terms:
            between = gz[k, z0] * d0
            f = gy[k, p0] * y0
            g = gx[k, p0] * x0
            store(k, p0, (f - pltpu.roll(f, width - 1, 1)) + (g - pltpu.roll(g, 7, 0)) + (between + db[k, p0] * v0))
            f = gy[k, p1] * y1
            g = gx[k, p1] * x1
            store(k, p1, (f - pltpu.roll(f, width - 1, 1)) + (g - pltpu.roll(g, 7, 0)) + (gz[k, 1] * d1 + db[k, p1] * v1 - between))

    def own_stencil(b, carry):
        def store(k, p, value):
            ak[b * TERMS + k, p] = value
        stencil((m[b, 0], m[b, 1], m[b, 2]), range(TERMS), store)
        return carry

    lax.fori_loop(0, TERMS, near_faces, 0)
    for copy in table_copies:
        copy.wait()
    for copy in to_sibling:
        copy.wait_recv()

    outer = jnp.logical_or(row == 0, row == 7)
    middle = jnp.logical_or(row == 3, row == 4)
    upper = jnp.logical_or(row == 0, row == 4)

    def spread(packed):
        return jnp.where(outer, packed, 0.0), jnp.where(outer, pltpu.roll(packed, 4, 0), 0.0)

    def inner_sum(slot, scale, totals):
        total0, total1 = totals
        for k in range(1, TERMS):
            for side in range(2):
                at = (k - 1) * 2 + side
                index = ti[at, slot] * TERMS + k
                weight = tf[at, slot] * scale
                total0 = total0 + weight * ak[index, 0]
                total1 = total1 + weight * ak[index, 1]
        return total0, total1

    def edge_sum(slot, first, scale, edges, faces, packed):
        for k in range(1, TERMS):
            at = first + (k - 1) * 2
            along = (tf[at, slot] * scale) * edges[ti[at, slot]] + (tf[at + 1, slot] * scale) * edges[ti[at + 1, slot]]
            packed = faces[k] * along if packed is None else packed + faces[k] * along
        return packed

    def item_copy(j):
        target = rb.at[j, pl.ds(0, 2)] if j < LATE else rl.at[j - LATE, pl.ds(0, 2)]
        return pltpu.make_async_remote_copy(
            sb.at[j], target, item_s.at[j], item_r.at[j], device_id=partner, device_id_type=MESH
        )

    def item_of(j):
        slot = ti[13, j]
        return slot, ti[14, slot], jnp.where(slot // CHIP == high, 1.0, 0.0).astype(f32)

    def slot_at(b):
        return high * CHIP + jnp.where(b < GROUP, core * GROUP + b, (1 - core) * GROUP + b - GROUP)

    def begin_item(j, carry):
        slot, place, ours = item_of(j)
        sb[j, 0], sb[j, 1] = inner_sum(slot, 1.0 - ours, (ours * m[place, 0], ours * m[place, 1]))
        return carry

    def early_item(j):
        slot, place, ours = item_of(j)
        totals = [ours * m[place, 0], ours * m[place, 1]]
        for k in range(1, TERMS):
            at = (k - 1) * 2
            weights = [tf[at + side, slot] * (1.0 - ours) for side in range(2)]
            places = [ti[at + side, slot] for side in range(2)]
            mixed = [weights[0] * m[places[0], p] + weights[1] * m[places[1], p] for p in range(3)]
            def store(_, p, value):
                totals[p] = totals[p] + value
            stencil(mixed, (k,), store)
        sb[j, 0], sb[j, 1] = totals

    for j in range(FIRST):
        early_item(j)
        item_copy(j).start()

    lax.fori_loop(0, CHIP, own_stencil, 0)
    for j in range(FIRST, EARLY):
        begin_item(j, 0)
        item_copy(j).start()
    lax.fori_loop(EARLY, EVENS, begin_item, 0)

    for there, side in downs:
        @pl.when(there)
        def _():
            for source in range(2):
                edge_copy(side, 0, source).wait_recv()

    def tile(top0, top1, bottom0, bottom1):
        return jnp.where(row == 0, top0, jnp.where(row == 7, bottom0, jnp.where(row == 4, top1, bottom1)))

    def own_edges(v0, v1):
        return jnp.where(outer, v0, pltpu.roll(v1, 4, 0))

    def arrived(ref, lead, r):
        return [ref[(side,) + lead + (pl.ds(r + p, 1), slice(None))] for side in range(2) for p in range(2)]

    left_out = jnp.logical_or(
        jnp.logical_and(low_seam, upper), jnp.logical_and(high_seam, jnp.logical_or(row == 7, row == 3))
    )
    for k in range(TERMS):
        faces = own_edges(c[k, 0], c[k, 1]) + tile(*arrived(er, (k // 2,), 10 + (k % 2) * 2))
        gh[k] = jnp.where(left_out, 0.0, 0.5 * faces)
    for b in range(CHIP):
        source = core if b < GROUP else 1 - core
        dh[b] = own_edges(m[b, 0], m[b, 1]) - tile(*arrived(er, (source,), (b % GROUP) * 2))

    tile_copy = pltpu.make_async_remote_copy(ts, tr, tile_s, tile_r, device_id=partner, device_id_type=MESH)

    for j in range(EARLY, EVENS):
        slot, place, ours = item_of(j)
        edge0, edge1 = spread(edge_sum(slot, 0, 1.0 - ours, dh, gh, None))
        sb[j, 0] = sb[j, 0] + edge0
        sb[j, 1] = sb[j, 1] + edge1
        item_copy(j).start()
        if j == EARLY:
            for t in range(2):
                pair = []
                for n in (2 * t, 2 * t + 1):
                    slot, _, ours = item_of(n)
                    packed = edge_sum(slot, 0, 1.0 - ours, dh, gh, None)
                    if LATE + n < EVENS:
                        _, place, ours = item_of(LATE + n)
                        packed = packed + ours * dh[place]
                    pair.append(packed)
                moved = jnp.where(jnp.logical_or(row == 1, row == 5), pltpu.roll(pair[1], 1, 0), pltpu.roll(pair[1], 7, 0))
                ts[t] = jnp.where(jnp.logical_or(outer, middle), pair[0], moved)
            tile_copy.start()

    def give(n, source, target):
        return pltpu.make_async_remote_copy(
            source, target, give_s.at[n], give_r.at[n], device_id=sibling, device_id_type=MESH
        )

    faces_copy = give(0, gh, ghf)
    tile_on = give(1, tr, trf)
    sums_copy = give(2, acc.at[pl.ds(GROUP, GROUP)], far)
    faces_copy.start()
    lax.fori_loop(0, TERMS, far_faces, 0)

    def local_sum(b, carry):
        slot = slot_at(b)
        weight = tf[13, slot]
        total0, total1 = inner_sum(slot, 1.0, (weight * ak[b * TERMS, 0], weight * ak[b * TERMS, 1]))
        edge0, edge1 = spread(edge_sum(slot, 0, 1.0, dh, gh, gh[0] * (weight * dh[b])))
        acc[b, 0], acc[b, 1] = total0 + edge0, total1 + edge1
        return carry

    lax.fori_loop(0, CHIP, local_sum, 0)

    def plane_copy(j):
        held, at = (rb, j) if j < LATE else (rl, j - LATE)
        return pltpu.make_async_remote_copy(
            held.at[at, pl.ds(1, 1)], held.at[at, pl.ds(2, 1)], plane_s.at[j], plane_r.at[j],
            device_id=sibling, device_id_type=MESH,
        )

    def outer_copy(n):
        return pltpu.make_async_remote_copy(
            rl.at[n, pl.ds(0, 1)], rl.at[n, pl.ds(3, 1)], outer_s.at[n], outer_r.at[n],
            device_id=sibling, device_id_type=MESH,
        )

    def edge_on(side, g):
        return pltpu.make_async_remote_copy(
            hs.at[side, g], hr.at[side, g], fwd_s.at[side, g], fwd_r.at[side, g],
            device_id=(mode, space + (1 if side == 0 else -1)), device_id_type=MESH,
        )

    def raw_stencil(j, carry):
        def store(k, p, value):
            akr[j * 3 + k - 1, p] = value
        stencil((rb[j, 0], rb[j, 1], rb[j, 2]), range(1, TERMS), store)
        return carry

    for g, members in enumerate(groups):
        for n, j in enumerate(members):
            item_copy(j).wait_recv()
            plane_copy(j).start()
            for side, r in ((0, 7), (1, 0)):
                for p in range(2):
                    hs[side, g, pl.ds(n * 2 + p, 1), :] = rb[j, p, pl.ds(r, 1), :]
        for there, side in ups:
            @pl.when(there)
            def _():
                edge_on(side, g).start()
        @pl.when(low_seam)
        def _():
            pl.semaphore_wait(ready, 4)
            for n in range(4):
                seam_copy(1, -1, n, mode).start()

        for j in members:
            plane_copy(j).wait_recv()
        lax.fori_loop(members[0], members[-1] + 1, raw_stencil, 0)
    def remote_sum(b, carry):
        slot = slot_at(b)
        index = ti[12, slot]
        soon = index < LATE
        weight = jnp.where(soon, tf[12, slot], 0.0)
        at = jnp.minimum(index, LATE - 1)
        total0, total1 = acc[b, 0] + weight * rb[at, 0], acc[b, 1] + weight * rb[at, 1]
        for cell in range(6):
            at = ti[6 + cell, slot]
            weight = jnp.where(at < LATE, tf[6 + cell, slot], 0.0)
            at = jnp.minimum(at, LATE - 1) * 3 + cell // 2
            total0 = total0 + weight * akr[at, 0]
            total1 = total1 + weight * akr[at, 1]
        acc[b, 0], acc[b, 1] = total0, total1
        return carry

    lax.fori_loop(0, CHIP, remote_sum, 0)

    def unpack(ref, target):
        for t in range(2):
            target[2 * t] = ref[t]
            target[2 * t + 1] = jnp.where(upper, pltpu.roll(ref[t], 7, 0), pltpu.roll(ref[t], 1, 0))

    tile_copy.wait_recv()
    tile_on.start()
    unpack(tr, drl)

    for g, members in enumerate(groups):
        for there, side in downs:
            @pl.when(there)
            def _():
                edge_on(side, g).wait_recv()
        for n, j in enumerate(members):
            dr[j] = own_edges(rb[j, 0], rb[j, 1]) - tile(*arrived(hr, (g,), n * 2))

    def remote_edges(b, carry):
        slot = slot_at(b)
        packed = None
        for k in range(1, TERMS):
            along = None
            for side in range(2):
                cell = 6 + (k - 1) * 2 + side
                at = ti[cell, slot]
                part = jnp.where(at < LATE, tf[cell, slot], 0.0) * dr[jnp.minimum(at, LATE - 1)]
                along = part if along is None else along + part
            packed = gh[k] * along if packed is None else packed + gh[k] * along
        edge0, edge1 = spread(packed)
        acc[b, 0] = acc[b, 0] + edge0
        acc[b, 1] = acc[b, 1] + edge1
        return carry

    lax.fori_loop(0, CHIP, remote_edges, 0)

    def seam_tiles(side, step):
        for source in range(4):
            seam_copy(side, step, 0, source).wait_recv()
        for source in range(2):
            pair_copy(side, 0, source).wait_recv()

        def rows(ref, lead, r):
            return jnp.where(outer, ref[lead, pl.ds(r, 1), :], ref[lead, pl.ds(r + 1, 1), :])

        beside = jnp.logical_or(
            jnp.logical_and(low_seam, upper), jnp.logical_and(high_seam, jnp.logical_or(row == 7, row == 3))
        )
        for k in range(TERMS):
            faces = own_edges(c[k, 0], c[k, 1]) + rows(sh, high * 2 + k // 2, 10 + (k % 2) * 2)
            gs[k] = jnp.where(beside, 0.5 * faces, 0.0)
        for b in range(CHIP):
            source = high * 2 + (core if b < GROUP else 1 - core)
            ds[b] = own_edges(m[b, 0], m[b, 1]) - rows(sh, source, (b % GROUP) * 2)
            ds[CHIP + b] = rows(se, b // GROUP, (b % GROUP) * 2) - rows(sh, (1 - high) * 2 + b // GROUP, (b % GROUP) * 2)

    def seam_sum(b):
        slot = slot_at(b)
        return edge_sum(slot, 16, 1.0, ds, gs, gs[0] * (tf[13, slot] * ds[b]))

    @pl.when(high_seam)
    def _():
        seam_tiles(0, 1)

        def seam_here(b, carry):
            edge0, edge1 = spread(seam_sum(b))
            acc[b, 0] = acc[b, 0] + edge0
            acc[b, 1] = acc[b, 1] + edge1
            return carry

        lax.fori_loop(0, CHIP, seam_here, 0)

    sums_copy.start()

    for n in range(ENDS):
        item_copy(LATE + n).wait_recv()
        plane_copy(LATE + n).start()
        outer_copy(n).start()

    def late_stencil(far_side, n):
        def store(k, p, value):
            akl[n * 3 + k - 1, p] = value
        near, mid, beyond = (3, 2, 1) if far_side else (0, 1, 2)
        stencil((rl[n, near], rl[n, mid], rl[n, beyond]), range(1, TERMS), store, far_side)

    for n in range(ENDS):
        plane_copy(LATE + n).wait_recv()
        late_stencil(False, n)
        outer_copy(n).wait_recv()
        late_stencil(True, n)
    faces_copy.wait_recv()
    tile_on.wait_recv()
    unpack(trf, drf)
    sums_copy.wait_recv()

    def late_sum(b, carry):
        slot = slot_at(b)
        index = ti[12, slot]
        late = index >= LATE
        weight = jnp.where(late, tf[12, slot], 0.0)
        at = jnp.maximum(index - LATE, 0)
        totals = [acc[b, 0], acc[b, 1], far[b, 1], far[b, 0]]
        totals = [total + weight * rl[at, p] for p, total in enumerate(totals)]
        weight = jnp.where(index < EARLY, tf[12, slot], 0.0)
        at = jnp.minimum(index, EARLY - 1)
        near_edge, far_edge = weight * drl[at], weight * drf[at]
        for n in range(ENDS):
            weight, term = jnp.float32(0.0), jnp.int32(0)
            for cell in range(6):
                found = ti[6 + cell, slot] == LATE + n
                weight = jnp.where(found, tf[6 + cell, slot], weight)
                term = jnp.where(found, cell // 2, term)
            totals = [total + weight * akl[n * 3 + term, p] for p, total in enumerate(totals)]
            near_edge = near_edge + gh[term + 1] * (weight * drl[n])
            far_edge = far_edge + ghf[term + 1] * (weight * drf[n])
        edges = spread(near_edge) + spread(far_edge)[::-1]
        for p in range(4):
            out[b, planes[p]] = totals[p] + edges[p]
        return carry

    lax.fori_loop(0, GROUP, late_sum, 0)

    @pl.when(low_seam)
    def _():
        seam_tiles(1, -1)

        def seam_for_sibling(b, carry):
            sp[b] = seam_sum(b + GROUP)
            return carry

        def seam_for_self(b, carry):
            for plane, edge in zip(planes, spread(seam_sum(b))):
                out[b, plane] = out[b, plane] + edge
            return carry

        def seam_from_sibling(b, carry):
            for plane, edge in zip(planes[::-1], spread(sq[b])):
                out[b, plane] = out[b, plane] + edge
            return carry

        lax.fori_loop(0, GROUP, seam_for_sibling, 0)
        seam_give = give(3, sp, sq)
        seam_give.start()
        lax.fori_loop(0, GROUP, seam_for_self, 0)
        seam_give.wait()
        lax.fori_loop(0, GROUP, seam_from_sibling, 0)

    for copy in to_sibling:
        copy.wait_send()
    for there, side in ups:
        @pl.when(there)
        def _():
            for other in range(2):
                edge_copy(side, other, core).wait_send()
            for g in range(len(groups)):
                edge_on(side, g).wait_send()

    for there, side, step in seams:
        @pl.when(there)
        def _():
            for other in range(2):
                pair_copy(side, other, core).wait_send()
            for n in range(4):
                seam_copy(side, step, n, mode).wait_send()

    for j in range(EVENS):
        item_copy(j).wait_send()
        plane_copy(j).wait_send()
    for n in range(ENDS):
        outer_copy(n).wait_send()
    for copy in (tile_copy, faces_copy, tile_on, sums_copy):
        copy.wait_send()


def galerkin(spaces, modes, coefs, coupling, values, assignment):
    width = modes.shape[3]
    f32 = jnp.float32
    groups = -(-LATE // 4)
    dma = pltpu.SemaphoreType.DMA
    vmem = pltpu.VMEM
    scratch = [
        vmem((CHIP, 4, 8, width), f32),
        vmem((TERMS, 4, 8, width), f32),
        vmem((2, 2, 16, width), f32),
        vmem((2, 2, 16, width), f32),
        vmem((TERMS, 4, 8, width), f32),
        vmem((TERMS, 4, 8, width), f32),
        vmem((TERMS, 4, 8, width), f32),
        vmem((TERMS, 4, 8, width), f32),
        vmem((TERMS, 8, width), f32),
        vmem((CHIP * TERMS, 2, 8, width), f32),
        vmem((CHIP, 8, width), f32),
        vmem((EVENS, 2, 8, width), f32),
        vmem((LATE, 3, 8, width), f32),
        vmem((2, 8, width), f32),
        vmem((2, 8, width), f32),
        vmem((2, groups, 8, width), f32),
        vmem((2, groups, 8, width), f32),
        vmem((LATE, 8, width), f32),
        vmem((LATE * 3, 2, 8, width), f32),
        vmem((CHIP, 2, 8, width), f32),
        vmem((4, 16, width), f32),
        vmem((2, 16, width), f32),
        vmem((SLOTS, 8, width), f32),
        vmem((TERMS, 8, width), f32),
        vmem((ENDS, 4, 8, width), f32),
        vmem((ENDS * 3, 4, 8, width), f32),
        vmem((EARLY, 8, width), f32),
        vmem((TERMS, 8, width), f32),
        vmem((2, 8, width), f32),
        vmem((EARLY, 8, width), f32),
        vmem((GROUP, 2, 8, width), f32),
        vmem((GROUP, 8, width), f32),
        vmem((GROUP, 8, width), f32),
        vmem(coupling.shape, jnp.int32),
        vmem(values.shape, f32),
        vmem(assignment.shape, jnp.int32),
        vmem((24, 128), jnp.int32),
        vmem((24, 128), f32),
        pltpu.SMEM((24, 128), jnp.int32),
        pltpu.SMEM((24, 128), f32),
        dma((2, 4)), dma((3,)), dma((2,)), dma((3,)), dma((3,)), dma((2, 2)), dma((2, 2)), dma((EVENS,)), dma((EVENS,)),
        dma(()), dma(()), dma((EVENS,)), dma((EVENS,)),
        dma((2, groups)), dma((2, groups)), dma((4,)), dma((4,)), dma((2,)), dma((2,)), dma((ENDS,)), dma((ENDS,)),
        dma((4,)), dma((4,)), pltpu.SemaphoreType.REGULAR,
    ]
    anywhere = pl.BlockSpec(memory_space=pltpu.HBM)
    return pl.pallas_call(
        functools.partial(kernel, spaces),
        out_shape=jax.ShapeDtypeStruct(modes.shape, f32),
        in_specs=[anywhere] * 5,
        out_specs=pl.BlockSpec(memory_space=pltpu.VMEM),
        scratch_shapes=scratch,
        compiler_params=pltpu.CompilerParams(
            collective_id=0, has_side_effects=True, vmem_limit_bytes=32 * 1024 * 1024
        ),
        name="galerkin",
    )(modes, coefs, coupling, values, assignment)


def solution(mesh):
    spaces = mesh.shape["space"]

    def shards(modes, coefficients, coupling, coupling_values, assignment):
        held = [
            pltpu.with_memory_space_constraint(x, pltpu.HBM)
            for x in (modes, coefficients, coupling.T, coupling_values[None], assignment[None])
        ]
        return galerkin(spaces, *held)

    in_specs = (P("mode", None, "space", None), P(None, None, "space", None), P(), P(), P())
    out_specs = P("mode", None, "space", None)
    return jax.shard_map(shards, mesh=mesh, in_specs=in_specs, out_specs=out_specs, check_vma=False)
```

```python
import functools

import jax
import jax.numpy as jnp
from jax import lax
from jax.experimental import pallas as pl
from jax.experimental.pallas import tpu as pltpu
from jax.sharding import PartitionSpec as P

MESH = pl.DeviceIdType.MESH
EVENS = 7
SLOTS = 20
GROUP = 5
CHIP = 10
TERMS = 4
ENTRIES = 80
EARLY = 3
LATE = 4
ENDS = EVENS - LATE
INF = 1 << 24


def tables(high, core, coupling, values, assignment):
    i32 = jnp.int32
    slot = lax.broadcasted_iota(i32, (1, SLOTS), 1)
    lane = lax.broadcasted_iota(i32, (SLOTS, SLOTS), 1)
    sub = lax.broadcasted_iota(i32, (SLOTS, SLOTS), 0)
    eye = lax.broadcasted_iota(i32, (ENTRIES, ENTRIES), 0) == lax.broadcasted_iota(i32, (ENTRIES, ENTRIES), 1)
    first, second, term = [jnp.sum(jnp.where(eye, coupling[n : n + 1], 0), axis=1, keepdims=True) for n in range(3)]
    value = jnp.sum(jnp.where(eye, values, 0.0), axis=1, keepdims=True)
    hit_first = first == assignment
    hit_second = second == assignment
    joined = jnp.logical_and(hit_first, term > 0)
    degree = jnp.sum(jnp.where(joined, 1, 0), axis=0, keepdims=True)
    five = jnp.where(degree == 5, 1, 0)
    by_five = jnp.sum(jnp.where(hit_second, five, 0), axis=1, keepdims=True)
    near_five = jnp.sum(jnp.where(joined, by_five, 0), axis=0, keepdims=True)
    even = jnp.where(jnp.logical_or(degree <= 2, near_five > 0), 0, 1)
    even_col = jnp.sum(jnp.where(lane == sub, even, 0), axis=1, keepdims=True)
    ahead = jnp.sum(jnp.where(sub < lane, even_col, 0), axis=0, keepdims=True)
    low = jnp.sum(jnp.where(sub < CHIP, even_col, 0), axis=0, keepdims=True)
    order0 = ahead
    order1 = jnp.where(slot < CHIP, ahead + (EVENS - low), ahead - low)
    mine = jnp.where(high == 0, order0, order1)
    theirs = jnp.where(high == 0, order1, order0)
    key_row = jnp.where(even > 0, mine, 99)
    key_col = jnp.sum(jnp.where(lane == sub, key_row, 0), axis=1, keepdims=True)
    slot_of = jnp.sum(jnp.where(key_col == lane, sub, 0), axis=0, keepdims=True)
    local = slot - high * CHIP
    here = jnp.logical_and(local >= 0, local < CHIP)
    place = jnp.where(core == 0, local, jnp.where(local < GROUP, local + GROUP, local - GROUP))
    place = jnp.where(here, place, CHIP + slot - (1 - high) * CHIP)
    code = slot * 8192 + theirs * 512 + place * 16 + even * 2 + jnp.where(here, 1, 0)
    code_of = jnp.sum(jnp.where(hit_second, code, 0), axis=1, keepdims=True)
    l_index, l_weight, r_index, r_weight, a_index, a_weight = [], [], [], [], [], []
    for k in range(1, TERMS):
        chosen = jnp.logical_and(hit_first, term == k)
        lower = jnp.min(jnp.where(chosen, code_of, INF), axis=0, keepdims=True)
        upper = jnp.max(jnp.where(chosen, code_of, -1), axis=0, keepdims=True)
        upper = jnp.where(upper == lower, -1, upper)
        for found, there in ((lower, lower < INF), (upper, upper >= 0)):
            weight = jnp.sum(jnp.where(jnp.logical_and(chosen, code_of == found), value, 0.0), axis=0, keepdims=True)
            is_here = (found % 2) == 1
            is_even = ((found // 2) % 2) == 1
            use_l = jnp.logical_and(there, is_here)
            use_r = jnp.logical_and(there, jnp.logical_and(is_even, jnp.logical_not(is_here)))
            l_index.append(jnp.where(use_l, (found // 16) % 32, 0))
            l_weight.append(jnp.where(use_l, weight, 0.0))
            r_index.append(jnp.where(use_r, (found // 512) % 16, 0))
            r_weight.append(jnp.where(use_r, weight, 0.0))
            a_index.append(jnp.where(there, (found // 16) % 32, 0))
            a_weight.append(jnp.where(there, weight, 0.0))
    diagonal = jnp.sum(jnp.where(jnp.logical_and(hit_first, term == 0), value, 0.0), axis=0, keepdims=True)
    zero_i = jnp.zeros_like(slot)
    zero_f = jnp.zeros_like(diagonal)
    theirs = jnp.where(even > 0, theirs, 0)
    place = jnp.where(here, place, 0)

    def within(rows, size):
        return [jnp.clip(x, 0, size - 1) for x in rows]

    l_index, r_index, a_index = within(l_index, CHIP), within(r_index, EVENS), within(a_index, SLOTS)
    ints = within([theirs], EVENS) + within([slot_of], SLOTS) + within([place], CHIP) + [zero_i]
    floats = [jnp.where(even > 0, 1.0, 0.0), diagonal, zero_f, zero_f]
    ints = jnp.concatenate(l_index + r_index + ints + a_index + [zero_i, zero_i], axis=0)
    floats = jnp.concatenate(l_weight + r_weight + floats + a_weight + [zero_f, zero_f], axis=0)
    return ints, floats


def kernel(
    spaces,
    modes, coefs, coupling, values, assignment, out,
    m, c, es, er, gy, gx, gz, db, gh, ak, dh, sb, rb, ts, tr, hs, hr, dr, akr, acc, sh, se, ds, gs,
    rl, akl, drl, ghf, trf, drf, far, sp, sq,
    cv, vv, av, tiv, tfv, ti, tf,
    load_sem, small_sem, table_sem, sib_s, sib_r, edge_s, edge_r, item_s, item_r, tile_s, tile_r, plane_s, plane_r,
    fwd_s, fwd_r, seam_s, seam_r, pair_s, pair_r, outer_s, outer_r, give_s, give_r, ready,
):
    f32, i32 = jnp.float32, jnp.int32
    mode, space = lax.axis_index("mode"), lax.axis_index("space")
    high, core = mode // 2, mode % 2
    half = spaces // 2
    low_seam, high_seam = space == half, space == half - 1
    seam = jnp.logical_or(low_seam, high_seam)
    has_low = jnp.logical_and(space > 0, jnp.logical_not(low_seam))
    has_high = jnp.logical_and(space < spaces - 1, jnp.logical_not(high_seam))
    seams = ((high_seam, 0, 1), (low_seam, 1, -1))
    sibling_mode = high * 2 + (1 - core)
    sibling = (sibling_mode, space)
    partner = ((1 - high) * 2 + core, space)
    diagonal = ((1 - high) * 2 + (1 - core), space)
    facing = (mode, sibling_mode, partner[0], diagonal[0])
    width = modes.shape[3]
    groups = [list(range(LATE))[i : i + 4] for i in range(0, LATE, 4)]
    planes = (3 * core, 1 + core, 2 - core, 3 - 3 * core)
    ups = ((has_high, 0), (has_low, 1))
    downs = ((has_low, 0), (has_high, 1))

    def signal(target):
        pl.semaphore_signal(barrier, inc=1, device_id=target, device_id_type=MESH)

    barrier = pltpu.get_barrier_semaphore()
    signal(sibling)
    signal(partner)
    for there, step in ((has_low, -1), (has_high, 1)):
        @pl.when(there)
        def _():
            for who in (mode, sibling_mode):
                signal((who, space + step))

    @pl.when(seam)
    def _():
        signal(diagonal)

    @pl.when(low_seam)
    def _():
        for who in facing:
            signal((who, space - 1))

    loads = []
    for at, plane in enumerate(planes):
        loads.append(pltpu.make_async_copy(modes.at[:, pl.ds(plane, 1)], m.at[pl.ds(0, GROUP), pl.ds(at, 1)], load_sem.at[0, at]))
        loads.append(pltpu.make_async_copy(coefs.at[:, pl.ds(plane, 1)], c.at[:, pl.ds(at, 1)], load_sem.at[1, at]))
    smalls = [
        pltpu.make_async_copy(source, target, small_sem.at[n])
        for n, (source, target) in enumerate(((coupling, cv), (values, vv), (assignment, av)))
    ]
    for copy in smalls + loads:
        copy.start()

    for copy in smalls:
        copy.wait()
    tiv[...] = jnp.zeros(tiv.shape, i32)
    tfv[...] = jnp.zeros(tfv.shape, f32)
    tiv[:, 0:SLOTS], tfv[:, 0:SLOTS] = tables(high, core, cv[...], vv[...], av[...])
    table_copies = [
        pltpu.make_async_copy(tiv, ti, table_sem.at[0]),
        pltpu.make_async_copy(tfv, tf, table_sem.at[1]),
    ]
    for copy in table_copies:
        copy.start()

    peers = 2 + 2 * has_low.astype(i32) + 2 * has_high.astype(i32) + seam.astype(i32) + 4 * high_seam.astype(i32)
    pl.semaphore_wait(barrier, peers)

    for copy in loads:
        copy.wait()

    to_sibling = [
        pltpu.make_async_remote_copy(
            m.at[pl.ds(0, GROUP), pl.ds(3 - at, 1)], m.at[pl.ds(GROUP, GROUP), pl.ds(at, 1)],
            sib_s.at[at], sib_r.at[at], device_id=sibling, device_id_type=MESH,
        )
        for at in range(3)
    ]
    for copy in to_sibling:
        copy.start()

    for side, row in ((0, 7), (1, 0)):
        for other, held in ((0, (0, 1)), (1, (3, 2))):
            for p in range(2):
                for i in range(GROUP):
                    es[side, other, pl.ds(i * 2 + p, 1), :] = m[i, held[p], pl.ds(row, 1), :]
                for kk in range(2):
                    es[side, other, pl.ds(10 + kk * 2 + p, 1), :] = c[2 * core + kk, held[p], pl.ds(row, 1), :]

    def edge_copy(side, other, source):
        who = mode if other == 0 else sibling_mode
        return pltpu.make_async_remote_copy(
            es.at[side, other], er.at[side, source], edge_s.at[side, other], edge_r.at[side, source],
            device_id=(who, space + (1 if side == 0 else -1)), device_id_type=MESH,
        )

    def seam_copy(side, step, n, source):
        return pltpu.make_async_remote_copy(
            es.at[side, n % 2], sh.at[source], seam_s.at[n], seam_r.at[source],
            device_id=(facing[n], space + step), device_id_type=MESH,
        )

    def pair_copy(side, other, source):
        return pltpu.make_async_remote_copy(
            es.at[side, other], se.at[source], pair_s.at[other], pair_r.at[source],
            device_id=partner if other == 0 else diagonal, device_id_type=MESH,
        )

    @pl.when(high_seam)
    def _():
        for who in facing:
            pl.semaphore_signal(ready, inc=1, device_id=(who, space + 1), device_id_type=MESH)
        for n in range(4):
            seam_copy(0, 1, n, mode).start()

    for there, side in ups:
        @pl.when(there)
        def _():
            for other in range(2):
                edge_copy(side, other, core).start()

    for there, side, _ in seams:
        @pl.when(there)
        def _():
            for other in range(2):
                pair_copy(side, other, core).start()

    for there, side in downs:
        @pl.when(jnp.logical_not(there))
        def _():
            er[side] = jnp.zeros(er.shape[1:], f32)
            hr[side] = jnp.zeros(hr.shape[1:], f32)

    row = lax.broadcasted_iota(i32, (8, width), 0)
    col = lax.broadcasted_iota(i32, (8, width), 1)

    def along_plane(k, p, carry):
        a = 0.5 * c[k, p]
        gy[k, p] = jnp.where(col == 0, 0.0, a + pltpu.roll(a, 1, 1))
        gx[k, p] = jnp.where(row == 0, 0.0, a + pltpu.roll(a, 1, 0))
        side = jnp.where(jnp.logical_or(col == 0, col == width - 1), 1.0, 0.0)
        db[k, p] = a * (side + carry)

    def near_faces(k, carry):
        along_plane(k, 0, 1.0)
        along_plane(k, 1, 0.0)
        gz[k, 0] = 0.5 * (c[k, 0] + c[k, 1])
        gz[k, 1] = 0.5 * (c[k, 1] + c[k, 2])
        return carry

    def far_faces(k, carry):
        along_plane(k, 3, 1.0)
        along_plane(k, 2, 0.0)
        gz[k, 2] = 0.5 * (c[k, 2] + c[k, 3])
        return carry

    def stencil(v, terms, store, far_side=False):
        p0, p1, z0 = (3, 2, 2) if far_side else (0, 1, 0)
        v0, v1, vh = v
        d0, d1 = v0 - v1, v1 - vh
        y0, y1 = v0 - pltpu.roll(v0, 1, 1), v1 - pltpu.roll(v1, 1, 1)
        x0, x1 = v0 - pltpu.roll(v0, 1, 0), v1 - pltpu.roll(v1, 1, 0)
        for k in terms:
            between = gz[k, z0] * d0
            f = gy[k, p0] * y0
            g = gx[k, p0] * x0
            store(k, p0, (f - pltpu.roll(f, width - 1, 1)) + (g - pltpu.roll(g, 7, 0)) + (between + db[k, p0] * v0))
            f = gy[k, p1] * y1
            g = gx[k, p1] * x1
            store(k, p1, (f - pltpu.roll(f, width - 1, 1)) + (g - pltpu.roll(g, 7, 0)) + (gz[k, 1] * d1 + db[k, p1] * v1 - between))

    def own_stencil(b, carry):
        def store(k, p, value):
            ak[b * TERMS + k, p] = value
        stencil((m[b, 0], m[b, 1], m[b, 2]), range(TERMS), store)
        return carry

    lax.fori_loop(0, TERMS, near_faces, 0)
    for copy in table_copies:
        copy.wait()
    for copy in to_sibling:
        copy.wait_recv()

    outer = jnp.logical_or(row == 0, row == 7)
    middle = jnp.logical_or(row == 3, row == 4)
    upper = jnp.logical_or(row == 0, row == 4)

    def spread(packed):
        return jnp.where(outer, packed, 0.0), jnp.where(outer, pltpu.roll(packed, 4, 0), 0.0)

    def inner_sum(slot, scale, totals):
        total0, total1 = totals
        for k in range(1, TERMS):
            for side in range(2):
                at = (k - 1) * 2 + side
                index = ti[at, slot] * TERMS + k
                weight = tf[at, slot] * scale
                total0 = total0 + weight * ak[index, 0]
                total1 = total1 + weight * ak[index, 1]
        return total0, total1

    def edge_sum(slot, first, scale, edges, faces, packed):
        for k in range(1, TERMS):
            at = first + (k - 1) * 2
            along = (tf[at, slot] * scale) * edges[ti[at, slot]] + (tf[at + 1, slot] * scale) * edges[ti[at + 1, slot]]
            packed = faces[k] * along if packed is None else packed + faces[k] * along
        return packed

    def item_copy(j):
        target = rb.at[j, pl.ds(0, 2)] if j < LATE else rl.at[j - LATE, pl.ds(0, 2)]
        return pltpu.make_async_remote_copy(
            sb.at[j], target, item_s.at[j], item_r.at[j], device_id=partner, device_id_type=MESH
        )

    def item_of(j):
        slot = ti[13, j]
        return slot, ti[14, slot], jnp.where(slot // CHIP == high, 1.0, 0.0).astype(f32)

    def slot_at(b):
        return high * CHIP + jnp.where(b < GROUP, core * GROUP + b, (1 - core) * GROUP + b - GROUP)

    def begin_item(j, carry):
        slot, place, ours = item_of(j)
        sb[j, 0], sb[j, 1] = inner_sum(slot, 1.0 - ours, (ours * m[place, 0], ours * m[place, 1]))
        return carry

    def early_item(j):
        slot, place, ours = item_of(j)
        totals = [ours * m[place, 0], ours * m[place, 1]]
        for k in range(1, TERMS):
            at = (k - 1) * 2
            weights = [tf[at + side, slot] * (1.0 - ours) for side in range(2)]
            places = [ti[at + side, slot] for side in range(2)]
            mixed = [weights[0] * m[places[0], p] + weights[1] * m[places[1], p] for p in range(3)]
            def store(_, p, value):
                totals[p] = totals[p] + value
            stencil(mixed, (k,), store)
        sb[j, 0], sb[j, 1] = totals

    for j in range(EARLY):
        early_item(j)
        item_copy(j).start()

    lax.fori_loop(0, CHIP, own_stencil, 0)
    lax.fori_loop(EARLY, EVENS, begin_item, 0)

    for there, side in downs:
        @pl.when(there)
        def _():
            for source in range(2):
                edge_copy(side, 0, source).wait_recv()

    def tile(top0, top1, bottom0, bottom1):
        return jnp.where(row == 0, top0, jnp.where(row == 7, bottom0, jnp.where(row == 4, top1, bottom1)))

    def own_edges(v0, v1):
        return jnp.where(outer, v0, pltpu.roll(v1, 4, 0))

    def arrived(ref, lead, r):
        return [ref[(side,) + lead + (pl.ds(r + p, 1), slice(None))] for side in range(2) for p in range(2)]

    left_out = jnp.logical_or(
        jnp.logical_and(low_seam, upper), jnp.logical_and(high_seam, jnp.logical_or(row == 7, row == 3))
    )
    for k in range(TERMS):
        faces = own_edges(c[k, 0], c[k, 1]) + tile(*arrived(er, (k // 2,), 10 + (k % 2) * 2))
        gh[k] = jnp.where(left_out, 0.0, 0.5 * faces)
    for b in range(CHIP):
        source = core if b < GROUP else 1 - core
        dh[b] = own_edges(m[b, 0], m[b, 1]) - tile(*arrived(er, (source,), (b % GROUP) * 2))

    def merged(one, two):
        which = lax.broadcasted_iota(i32, one.shape, 0)
        stay = (which % 4 == 0) | (which % 4 == 3)
        moved = jnp.where(which % 4 == 1, pltpu.roll(two, 1, 0), pltpu.roll(two, 7, 0))
        return jnp.where(stay, one, moved)

    def second(both):
        which = lax.broadcasted_iota(i32, both.shape, 0)
        return jnp.where(which % 4 == 0, pltpu.roll(both, 7, 0), pltpu.roll(both, 1, 0))

    tile_copy = pltpu.make_async_remote_copy(ts, tr, tile_s, tile_r, device_id=partner, device_id_type=MESH)

    for j in range(EARLY, EVENS):
        slot, place, ours = item_of(j)
        edge0, edge1 = spread(edge_sum(slot, 0, 1.0 - ours, dh, gh, None))
        sb[j, 0] = sb[j, 0] + edge0
        sb[j, 1] = sb[j, 1] + edge1
        item_copy(j).start()
        if j == EARLY:
            parts = []
            for n in range(EARLY):
                slot, _, ours = item_of(n)
                packed = edge_sum(slot, 0, 1.0 - ours, dh, gh, None)
                _, place, ours = item_of(LATE + n)
                parts.append(packed + ours * dh[place])
            ts[:, pl.ds(0, width)] = merged(parts[0], parts[1])
            ts[:, pl.ds(width, width // 2)] = merged(parts[2][:, : width // 2], parts[2][:, width // 2 :])
            tile_copy.start()

    def give(n, source, target):
        return pltpu.make_async_remote_copy(
            source, target, give_s.at[n], give_r.at[n], device_id=sibling, device_id_type=MESH
        )

    faces_copy = give(0, gh, ghf)
    tile_on = give(1, tr, trf)
    sums_copy = give(2, acc.at[pl.ds(GROUP, GROUP)], far)
    faces_copy.start()
    lax.fori_loop(0, TERMS, far_faces, 0)

    def local_sum(b, carry):
        slot = slot_at(b)
        weight = tf[13, slot]
        total0, total1 = inner_sum(slot, 1.0, (weight * ak[b * TERMS, 0], weight * ak[b * TERMS, 1]))
        edge0, edge1 = spread(edge_sum(slot, 0, 1.0, dh, gh, gh[0] * (weight * dh[b])))
        acc[b, 0], acc[b, 1] = total0 + edge0, total1 + edge1
        return carry

    lax.fori_loop(0, CHIP, local_sum, 0)

    def plane_copy(j):
        held, at = (rb, j) if j < LATE else (rl, j - LATE)
        return pltpu.make_async_remote_copy(
            held.at[at, pl.ds(1, 1)], held.at[at, pl.ds(2, 1)], plane_s.at[j], plane_r.at[j],
            device_id=sibling, device_id_type=MESH,
        )

    def outer_copy(n):
        return pltpu.make_async_remote_copy(
            rl.at[n, pl.ds(0, 1)], rl.at[n, pl.ds(3, 1)], outer_s.at[n], outer_r.at[n],
            device_id=sibling, device_id_type=MESH,
        )

    def edge_on(side, g):
        return pltpu.make_async_remote_copy(
            hs.at[side, g], hr.at[side, g], fwd_s.at[side, g], fwd_r.at[side, g],
            device_id=(mode, space + (1 if side == 0 else -1)), device_id_type=MESH,
        )

    def raw_stencil(j, carry):
        def store(k, p, value):
            akr[j * 3 + k - 1, p] = value
        stencil((rb[j, 0], rb[j, 1], rb[j, 2]), range(1, TERMS), store)
        return carry

    for g, members in enumerate(groups):
        for n, j in enumerate(members):
            item_copy(j).wait_recv()
            plane_copy(j).start()
            for side, r in ((0, 7), (1, 0)):
                for p in range(2):
                    hs[side, g, pl.ds(n * 2 + p, 1), :] = rb[j, p, pl.ds(r, 1), :]
        for there, side in ups:
            @pl.when(there)
            def _():
                edge_on(side, g).start()
        @pl.when(low_seam)
        def _():
            pl.semaphore_wait(ready, 4)
            for n in range(4):
                seam_copy(1, -1, n, mode).start()

        for j in members:
            plane_copy(j).wait_recv()
        lax.fori_loop(members[0], members[-1] + 1, raw_stencil, 0)
    def remote_sum(b, carry):
        slot = slot_at(b)
        index = ti[12, slot]
        soon = index < LATE
        weight = jnp.where(soon, tf[12, slot], 0.0)
        at = jnp.minimum(index, LATE - 1)
        total0, total1 = acc[b, 0] + weight * rb[at, 0], acc[b, 1] + weight * rb[at, 1]
        for cell in range(6):
            at = ti[6 + cell, slot]
            weight = jnp.where(at < LATE, tf[6 + cell, slot], 0.0)
            at = jnp.minimum(at, LATE - 1) * 3 + cell // 2
            total0 = total0 + weight * akr[at, 0]
            total1 = total1 + weight * akr[at, 1]
        acc[b, 0], acc[b, 1] = total0, total1
        return carry

    lax.fori_loop(0, CHIP, remote_sum, 0)

    def unpack(ref, target):
        target[0] = ref[:, pl.ds(0, width)]
        target[1] = second(ref[:, pl.ds(0, width)])
        target[2, :, pl.ds(0, width // 2)] = ref[:, pl.ds(width, width // 2)]
        target[2, :, pl.ds(width // 2, width // 2)] = second(ref[:, pl.ds(width, width // 2)])

    tile_copy.wait_recv()
    tile_on.start()
    unpack(tr, drl)

    for g, members in enumerate(groups):
        for there, side in downs:
            @pl.when(there)
            def _():
                edge_on(side, g).wait_recv()
        for n, j in enumerate(members):
            dr[j] = own_edges(rb[j, 0], rb[j, 1]) - tile(*arrived(hr, (g,), n * 2))

    def remote_edges(b, carry):
        slot = slot_at(b)
        packed = None
        for k in range(1, TERMS):
            along = None
            for side in range(2):
                cell = 6 + (k - 1) * 2 + side
                at = ti[cell, slot]
                part = jnp.where(at < LATE, tf[cell, slot], 0.0) * dr[jnp.minimum(at, LATE - 1)]
                along = part if along is None else along + part
            packed = gh[k] * along if packed is None else packed + gh[k] * along
        edge0, edge1 = spread(packed)
        acc[b, 0] = acc[b, 0] + edge0
        acc[b, 1] = acc[b, 1] + edge1
        return carry

    lax.fori_loop(0, CHIP, remote_edges, 0)

    def seam_tiles(side, step):
        for source in range(4):
            seam_copy(side, step, 0, source).wait_recv()
        for source in range(2):
            pair_copy(side, 0, source).wait_recv()

        def rows(ref, lead, r):
            return jnp.where(outer, ref[lead, pl.ds(r, 1), :], ref[lead, pl.ds(r + 1, 1), :])

        beside = jnp.logical_or(
            jnp.logical_and(low_seam, upper), jnp.logical_and(high_seam, jnp.logical_or(row == 7, row == 3))
        )
        for k in range(TERMS):
            faces = own_edges(c[k, 0], c[k, 1]) + rows(sh, high * 2 + k // 2, 10 + (k % 2) * 2)
            gs[k] = jnp.where(beside, 0.5 * faces, 0.0)
        for b in range(CHIP):
            source = high * 2 + (core if b < GROUP else 1 - core)
            ds[b] = own_edges(m[b, 0], m[b, 1]) - rows(sh, source, (b % GROUP) * 2)
            ds[CHIP + b] = rows(se, b // GROUP, (b % GROUP) * 2) - rows(sh, (1 - high) * 2 + b // GROUP, (b % GROUP) * 2)

    def seam_sum(b):
        slot = slot_at(b)
        return edge_sum(slot, 16, 1.0, ds, gs, gs[0] * (tf[13, slot] * ds[b]))

    @pl.when(high_seam)
    def _():
        seam_tiles(0, 1)

        def seam_here(b, carry):
            edge0, edge1 = spread(seam_sum(b))
            acc[b, 0] = acc[b, 0] + edge0
            acc[b, 1] = acc[b, 1] + edge1
            return carry

        lax.fori_loop(0, CHIP, seam_here, 0)

    sums_copy.start()

    for n in range(ENDS):
        item_copy(LATE + n).wait_recv()
        plane_copy(LATE + n).start()
        outer_copy(n).start()

    def late_stencil(far_side, n):
        def store(k, p, value):
            akl[n * 3 + k - 1, p] = value
        near, mid, beyond = (3, 2, 1) if far_side else (0, 1, 2)
        stencil((rl[n, near], rl[n, mid], rl[n, beyond]), range(1, TERMS), store, far_side)

    for n in range(ENDS):
        plane_copy(LATE + n).wait_recv()
        late_stencil(False, n)
        outer_copy(n).wait_recv()
        late_stencil(True, n)
    faces_copy.wait_recv()
    tile_on.wait_recv()
    unpack(trf, drf)
    sums_copy.wait_recv()

    def late_sum(b, carry):
        slot = slot_at(b)
        index = ti[12, slot]
        late = index >= LATE
        weight = jnp.where(late, tf[12, slot], 0.0)
        at = jnp.maximum(index - LATE, 0)
        totals = [acc[b, 0], acc[b, 1], far[b, 1], far[b, 0]]
        totals = [total + weight * rl[at, p] for p, total in enumerate(totals)]
        weight = jnp.where(index < EARLY, tf[12, slot], 0.0)
        at = jnp.minimum(index, EARLY - 1)
        near_edge, far_edge = weight * drl[at], weight * drf[at]
        for n in range(ENDS):
            weight, term = jnp.float32(0.0), jnp.int32(0)
            for cell in range(6):
                found = ti[6 + cell, slot] == LATE + n
                weight = jnp.where(found, tf[6 + cell, slot], weight)
                term = jnp.where(found, cell // 2, term)
            totals = [total + weight * akl[n * 3 + term, p] for p, total in enumerate(totals)]
            near_edge = near_edge + gh[term + 1] * (weight * drl[n])
            far_edge = far_edge + ghf[term + 1] * (weight * drf[n])
        edges = spread(near_edge) + spread(far_edge)[::-1]
        for p in range(4):
            out[b, planes[p]] = totals[p] + edges[p]
        return carry

    lax.fori_loop(0, GROUP, late_sum, 0)

    @pl.when(low_seam)
    def _():
        seam_tiles(1, -1)

        def seam_for_sibling(b, carry):
            sp[b] = seam_sum(b + GROUP)
            return carry

        def seam_for_self(b, carry):
            for plane, edge in zip(planes, spread(seam_sum(b))):
                out[b, plane] = out[b, plane] + edge
            return carry

        def seam_from_sibling(b, carry):
            for plane, edge in zip(planes[::-1], spread(sq[b])):
                out[b, plane] = out[b, plane] + edge
            return carry

        lax.fori_loop(0, GROUP, seam_for_sibling, 0)
        seam_give = give(3, sp, sq)
        seam_give.start()
        lax.fori_loop(0, GROUP, seam_for_self, 0)
        seam_give.wait()
        lax.fori_loop(0, GROUP, seam_from_sibling, 0)

    for copy in to_sibling:
        copy.wait_send()
    for there, side in ups:
        @pl.when(there)
        def _():
            for other in range(2):
                edge_copy(side, other, core).wait_send()
            for g in range(len(groups)):
                edge_on(side, g).wait_send()

    for there, side, step in seams:
        @pl.when(there)
        def _():
            for other in range(2):
                pair_copy(side, other, core).wait_send()
            for n in range(4):
                seam_copy(side, step, n, mode).wait_send()

    for j in range(EVENS):
        item_copy(j).wait_send()
        plane_copy(j).wait_send()
    for n in range(ENDS):
        outer_copy(n).wait_send()
    for copy in (tile_copy, faces_copy, tile_on, sums_copy):
        copy.wait_send()


def galerkin(spaces, modes, coefs, coupling, values, assignment):
    width = modes.shape[3]
    f32 = jnp.float32
    groups = -(-LATE // 4)
    dma = pltpu.SemaphoreType.DMA
    vmem = pltpu.VMEM
    scratch = [
        vmem((CHIP, 4, 8, width), f32),
        vmem((TERMS, 4, 8, width), f32),
        vmem((2, 2, 16, width), f32),
        vmem((2, 2, 16, width), f32),
        vmem((TERMS, 4, 8, width), f32),
        vmem((TERMS, 4, 8, width), f32),
        vmem((TERMS, 4, 8, width), f32),
        vmem((TERMS, 4, 8, width), f32),
        vmem((TERMS, 8, width), f32),
        vmem((CHIP * TERMS, 2, 8, width), f32),
        vmem((CHIP, 8, width), f32),
        vmem((EVENS, 2, 8, width), f32),
        vmem((LATE, 3, 8, width), f32),
        vmem((8, width + width // 2), f32),
        vmem((8, width + width // 2), f32),
        vmem((2, groups, 8, width), f32),
        vmem((2, groups, 8, width), f32),
        vmem((LATE, 8, width), f32),
        vmem((LATE * 3, 2, 8, width), f32),
        vmem((CHIP, 2, 8, width), f32),
        vmem((4, 16, width), f32),
        vmem((2, 16, width), f32),
        vmem((SLOTS, 8, width), f32),
        vmem((TERMS, 8, width), f32),
        vmem((ENDS, 4, 8, width), f32),
        vmem((ENDS * 3, 4, 8, width), f32),
        vmem((EARLY, 8, width), f32),
        vmem((TERMS, 8, width), f32),
        vmem((8, width + width // 2), f32),
        vmem((EARLY, 8, width), f32),
        vmem((GROUP, 2, 8, width), f32),
        vmem((GROUP, 8, width), f32),
        vmem((GROUP, 8, width), f32),
        vmem(coupling.shape, jnp.int32),
        vmem(values.shape, f32),
        vmem(assignment.shape, jnp.int32),
        vmem((24, 128), jnp.int32),
        vmem((24, 128), f32),
        pltpu.SMEM((24, 128), jnp.int32),
        pltpu.SMEM((24, 128), f32),
        dma((2, 4)), dma((3,)), dma((2,)), dma((3,)), dma((3,)), dma((2, 2)), dma((2, 2)), dma((EVENS,)), dma((EVENS,)),
        dma(()), dma(()), dma((EVENS,)), dma((EVENS,)),
        dma((2, groups)), dma((2, groups)), dma((4,)), dma((4,)), dma((2,)), dma((2,)), dma((ENDS,)), dma((ENDS,)),
        dma((4,)), dma((4,)), pltpu.SemaphoreType.REGULAR,
    ]
    anywhere = pl.BlockSpec(memory_space=pltpu.HBM)
    return pl.pallas_call(
        functools.partial(kernel, spaces),
        out_shape=jax.ShapeDtypeStruct(modes.shape, f32),
        in_specs=[anywhere] * 5,
        out_specs=pl.BlockSpec(memory_space=pltpu.VMEM),
        scratch_shapes=scratch,
        compiler_params=pltpu.CompilerParams(
            collective_id=0, has_side_effects=True, vmem_limit_bytes=32 * 1024 * 1024
        ),
        name="galerkin",
    )(modes, coefs, coupling, values, assignment)


def solution(mesh):
    spaces = mesh.shape["space"]

    def shards(modes, coefficients, coupling, coupling_values, assignment):
        held = [
            pltpu.with_memory_space_constraint(x, pltpu.HBM)
            for x in (modes, coefficients, coupling.T, coupling_values[None], assignment[None])
        ]
        return galerkin(spaces, *held)

    in_specs = (P("mode", None, "space", None), P(None, None, "space", None), P(), P(), P())
    out_specs = P("mode", None, "space", None)
    return jax.shard_map(shards, mesh=mesh, in_specs=in_specs, out_specs=out_specs, check_vma=False)
```

```python
import functools

import jax
import jax.numpy as jnp
from jax import lax
from jax.experimental import pallas as pl
from jax.experimental.pallas import tpu as pltpu
from jax.sharding import PartitionSpec as P

MESH = pl.DeviceIdType.MESH
EVENS = 7
SLOTS = 20
GROUP = 5
CHIP = 10
TERMS = 4
ENTRIES = 80
EARLY = 3
LATE = 4
ENDS = EVENS - LATE
INF = 1 << 24


def tables(high, core, coupling, values, assignment):
    i32 = jnp.int32
    slot = lax.broadcasted_iota(i32, (1, SLOTS), 1)
    lane = lax.broadcasted_iota(i32, (SLOTS, SLOTS), 1)
    sub = lax.broadcasted_iota(i32, (SLOTS, SLOTS), 0)
    eye = lax.broadcasted_iota(i32, (ENTRIES, ENTRIES), 0) == lax.broadcasted_iota(i32, (ENTRIES, ENTRIES), 1)
    first, second, term = [jnp.sum(jnp.where(eye, coupling[n : n + 1], 0), axis=1, keepdims=True) for n in range(3)]
    value = jnp.sum(jnp.where(eye, values, 0.0), axis=1, keepdims=True)
    hit_first = first == assignment
    hit_second = second == assignment
    joined = jnp.logical_and(hit_first, term > 0)
    degree = jnp.sum(jnp.where(joined, 1, 0), axis=0, keepdims=True)
    five = jnp.where(degree == 5, 1, 0)
    by_five = jnp.sum(jnp.where(hit_second, five, 0), axis=1, keepdims=True)
    near_five = jnp.sum(jnp.where(joined, by_five, 0), axis=0, keepdims=True)
    even = jnp.where(jnp.logical_or(degree <= 2, near_five > 0), 0, 1)
    even_col = jnp.sum(jnp.where(lane == sub, even, 0), axis=1, keepdims=True)
    ahead = jnp.sum(jnp.where(sub < lane, even_col, 0), axis=0, keepdims=True)
    low = jnp.sum(jnp.where(sub < CHIP, even_col, 0), axis=0, keepdims=True)
    order0 = ahead
    order1 = jnp.where(slot < CHIP, ahead + (EVENS - low), ahead - low)
    mine = jnp.where(high == 0, order0, order1)
    theirs = jnp.where(high == 0, order1, order0)
    key_row = jnp.where(even > 0, mine, 99)
    key_col = jnp.sum(jnp.where(lane == sub, key_row, 0), axis=1, keepdims=True)
    slot_of = jnp.sum(jnp.where(key_col == lane, sub, 0), axis=0, keepdims=True)
    local = slot - high * CHIP
    here = jnp.logical_and(local >= 0, local < CHIP)
    place = jnp.where(core == 0, local, jnp.where(local < GROUP, local + GROUP, local - GROUP))
    place = jnp.where(here, place, CHIP + slot - (1 - high) * CHIP)
    code = slot * 8192 + theirs * 512 + place * 16 + even * 2 + jnp.where(here, 1, 0)
    code_of = jnp.sum(jnp.where(hit_second, code, 0), axis=1, keepdims=True)
    l_index, l_weight, r_index, r_weight, a_index, a_weight = [], [], [], [], [], []
    for k in range(1, TERMS):
        chosen = jnp.logical_and(hit_first, term == k)
        lower = jnp.min(jnp.where(chosen, code_of, INF), axis=0, keepdims=True)
        upper = jnp.max(jnp.where(chosen, code_of, -1), axis=0, keepdims=True)
        upper = jnp.where(upper == lower, -1, upper)
        for found, there in ((lower, lower < INF), (upper, upper >= 0)):
            weight = jnp.sum(jnp.where(jnp.logical_and(chosen, code_of == found), value, 0.0), axis=0, keepdims=True)
            is_here = (found % 2) == 1
            is_even = ((found // 2) % 2) == 1
            use_l = jnp.logical_and(there, is_here)
            use_r = jnp.logical_and(there, jnp.logical_and(is_even, jnp.logical_not(is_here)))
            l_index.append(jnp.where(use_l, (found // 16) % 32, 0))
            l_weight.append(jnp.where(use_l, weight, 0.0))
            r_index.append(jnp.where(use_r, (found // 512) % 16, 0))
            r_weight.append(jnp.where(use_r, weight, 0.0))
            a_index.append(jnp.where(there, (found // 16) % 32, 0))
            a_weight.append(jnp.where(there, weight, 0.0))
    diagonal = jnp.sum(jnp.where(jnp.logical_and(hit_first, term == 0), value, 0.0), axis=0, keepdims=True)
    zero_i = jnp.zeros_like(slot)
    zero_f = jnp.zeros_like(diagonal)
    theirs = jnp.where(even > 0, theirs, 0)
    place = jnp.where(here, place, 0)

    def within(rows, size):
        return [jnp.clip(x, 0, size - 1) for x in rows]

    l_index, r_index, a_index = within(l_index, CHIP), within(r_index, EVENS), within(a_index, SLOTS)
    ints = within([theirs], EVENS) + within([slot_of], SLOTS) + within([place], CHIP) + [zero_i]
    floats = [jnp.where(even > 0, 1.0, 0.0), diagonal, zero_f, zero_f]
    ints = jnp.concatenate(l_index + r_index + ints + a_index + [zero_i, zero_i], axis=0)
    floats = jnp.concatenate(l_weight + r_weight + floats + a_weight + [zero_f, zero_f], axis=0)
    return ints, floats


def kernel(
    spaces,
    modes, coefs, coupling, values, assignment, out,
    m, c, es, er, gy, gx, gz, db, gh, ak, dh, sb, rb, ts, tr, hs, hr, dr, akr, acc, sh, se, ds, gs,
    rl, akl, drl, ghf, trf, drf, far, sp, sq,
    cv, vv, av, tiv, tfv, ti, tf,
    load_sem, small_sem, table_sem, sib_s, sib_r, edge_s, edge_r, item_s, item_r, tile_s, tile_r, plane_s, plane_r,
    fwd_s, fwd_r, seam_s, seam_r, pair_s, pair_r, outer_s, outer_r, give_s, give_r, ready, inner_s, inner_r,
):
    f32, i32 = jnp.float32, jnp.int32
    mode, space = lax.axis_index("mode"), lax.axis_index("space")
    high, core = mode // 2, mode % 2
    half = spaces // 2
    low_seam, high_seam = space == half, space == half - 1
    seam = jnp.logical_or(low_seam, high_seam)
    has_low = jnp.logical_and(space > 0, jnp.logical_not(low_seam))
    has_high = jnp.logical_and(space < spaces - 1, jnp.logical_not(high_seam))
    seams = ((high_seam, 0, 1), (low_seam, 1, -1))
    sibling_mode = high * 2 + (1 - core)
    sibling = (sibling_mode, space)
    partner = ((1 - high) * 2 + core, space)
    diagonal = ((1 - high) * 2 + (1 - core), space)
    facing = (mode, sibling_mode, partner[0], diagonal[0])
    width = modes.shape[3]
    groups = [list(range(LATE))[i : i + 4] for i in range(0, LATE, 4)]
    planes = (3 * core, 1 + core, 2 - core, 3 - 3 * core)
    ups = ((has_high, 0), (has_low, 1))
    downs = ((has_low, 0), (has_high, 1))

    def signal(target):
        pl.semaphore_signal(barrier, inc=1, device_id=target, device_id_type=MESH)

    barrier = pltpu.get_barrier_semaphore()
    signal(sibling)
    signal(partner)
    for there, step in ((has_low, -1), (has_high, 1)):
        @pl.when(there)
        def _():
            for who in (mode, sibling_mode):
                signal((who, space + step))

    @pl.when(seam)
    def _():
        signal(diagonal)

    @pl.when(low_seam)
    def _():
        for who in facing:
            signal((who, space - 1))

    loads = []
    for at, plane in enumerate(planes):
        loads.append(pltpu.make_async_copy(modes.at[:, pl.ds(plane, 1)], m.at[pl.ds(0, GROUP), pl.ds(at, 1)], load_sem.at[0, at]))
        loads.append(pltpu.make_async_copy(coefs.at[:, pl.ds(plane, 1)], c.at[:, pl.ds(at, 1)], load_sem.at[1, at]))
    smalls = [
        pltpu.make_async_copy(source, target, small_sem.at[n])
        for n, (source, target) in enumerate(((coupling, cv), (values, vv), (assignment, av)))
    ]
    for copy in smalls + loads:
        copy.start()

    for copy in smalls:
        copy.wait()
    tiv[...] = jnp.zeros(tiv.shape, i32)
    tfv[...] = jnp.zeros(tfv.shape, f32)
    tiv[:, 0:SLOTS], tfv[:, 0:SLOTS] = tables(high, core, cv[...], vv[...], av[...])
    table_copies = [
        pltpu.make_async_copy(tiv, ti, table_sem.at[0]),
        pltpu.make_async_copy(tfv, tf, table_sem.at[1]),
    ]
    for copy in table_copies:
        copy.start()

    peers = 2 + 2 * has_low.astype(i32) + 2 * has_high.astype(i32) + seam.astype(i32) + 4 * high_seam.astype(i32)
    pl.semaphore_wait(barrier, peers)

    for copy in loads:
        copy.wait()

    to_sibling = [
        pltpu.make_async_remote_copy(
            m.at[pl.ds(0, GROUP), pl.ds(3 - at, 1)], m.at[pl.ds(GROUP, GROUP), pl.ds(at, 1)],
            sib_s.at[at], sib_r.at[at], device_id=sibling, device_id_type=MESH,
        )
        for at in range(3)
    ]
    for copy in to_sibling:
        copy.start()

    for side, row in ((0, 7), (1, 0)):
        for other, held in ((0, (0, 1)), (1, (3, 2))):
            for p in range(2):
                for i in range(GROUP):
                    es[side, other, pl.ds(i * 2 + p, 1), :] = m[i, held[p], pl.ds(row, 1), :]
                for kk in range(2):
                    es[side, other, pl.ds(10 + kk * 2 + p, 1), :] = c[2 * core + kk, held[p], pl.ds(row, 1), :]

    def edge_copy(side, other, source):
        who = mode if other == 0 else sibling_mode
        return pltpu.make_async_remote_copy(
            es.at[side, other], er.at[side, source], edge_s.at[side, other], edge_r.at[side, source],
            device_id=(who, space + (1 if side == 0 else -1)), device_id_type=MESH,
        )

    def seam_copy(side, step, n, source):
        return pltpu.make_async_remote_copy(
            es.at[side, n % 2], sh.at[source], seam_s.at[n], seam_r.at[source],
            device_id=(facing[n], space + step), device_id_type=MESH,
        )

    def pair_copy(side, other, source):
        return pltpu.make_async_remote_copy(
            es.at[side, other], se.at[source], pair_s.at[other], pair_r.at[source],
            device_id=partner if other == 0 else diagonal, device_id_type=MESH,
        )

    @pl.when(high_seam)
    def _():
        for who in facing:
            pl.semaphore_signal(ready, inc=1, device_id=(who, space + 1), device_id_type=MESH)
        for n in range(4):
            seam_copy(0, 1, n, mode).start()

    for there, side in ups:
        @pl.when(there)
        def _():
            for other in range(2):
                edge_copy(side, other, core).start()

    for there, side, _ in seams:
        @pl.when(there)
        def _():
            for other in range(2):
                pair_copy(side, other, core).start()

    for there, side in downs:
        @pl.when(jnp.logical_not(there))
        def _():
            er[side] = jnp.zeros(er.shape[1:], f32)
            hr[side] = jnp.zeros(hr.shape[1:], f32)

    row = lax.broadcasted_iota(i32, (8, width), 0)
    col = lax.broadcasted_iota(i32, (8, width), 1)

    def along_plane(k, p, carry):
        a = 0.5 * c[k, p]
        gy[k, p] = jnp.where(col == 0, 0.0, a + pltpu.roll(a, 1, 1))
        gx[k, p] = jnp.where(row == 0, 0.0, a + pltpu.roll(a, 1, 0))
        side = jnp.where(jnp.logical_or(col == 0, col == width - 1), 1.0, 0.0)
        db[k, p] = a * (side + carry)

    def near_faces(k, carry):
        along_plane(k, 0, 1.0)
        along_plane(k, 1, 0.0)
        gz[k, 0] = 0.5 * (c[k, 0] + c[k, 1])
        gz[k, 1] = 0.5 * (c[k, 1] + c[k, 2])
        return carry

    def far_faces(k, carry):
        along_plane(k, 3, 1.0)
        along_plane(k, 2, 0.0)
        gz[k, 2] = 0.5 * (c[k, 2] + c[k, 3])
        return carry

    def stencil(v, terms, store, far_side=False):
        p0, p1, z0 = (3, 2, 2) if far_side else (0, 1, 0)
        v0, v1, vh = v
        d0, d1 = v0 - v1, v1 - vh
        y0, y1 = v0 - pltpu.roll(v0, 1, 1), v1 - pltpu.roll(v1, 1, 1)
        x0, x1 = v0 - pltpu.roll(v0, 1, 0), v1 - pltpu.roll(v1, 1, 0)
        for k in terms:
            between = gz[k, z0] * d0
            f = gy[k, p0] * y0
            g = gx[k, p0] * x0
            store(k, p0, (f - pltpu.roll(f, width - 1, 1)) + (g - pltpu.roll(g, 7, 0)) + (between + db[k, p0] * v0))
            f = gy[k, p1] * y1
            g = gx[k, p1] * x1
            store(k, p1, (f - pltpu.roll(f, width - 1, 1)) + (g - pltpu.roll(g, 7, 0)) + (gz[k, 1] * d1 + db[k, p1] * v1 - between))

    def own_stencil(b, carry):
        def store(k, p, value):
            ak[b * TERMS + k, p] = value
        stencil((m[b, 0], m[b, 1], m[b, 2]), range(TERMS), store)
        return carry

    lax.fori_loop(0, TERMS, near_faces, 0)
    for copy in table_copies:
        copy.wait()
    for copy in to_sibling:
        copy.wait_recv()

    outer = jnp.logical_or(row == 0, row == 7)
    middle = jnp.logical_or(row == 3, row == 4)
    upper = jnp.logical_or(row == 0, row == 4)

    def spread(packed):
        return jnp.where(outer, packed, 0.0), jnp.where(outer, pltpu.roll(packed, 4, 0), 0.0)

    def inner_sum(slot, scale, totals):
        total0, total1 = totals
        for k in range(1, TERMS):
            for side in range(2):
                at = (k - 1) * 2 + side
                index = ti[at, slot] * TERMS + k
                weight = tf[at, slot] * scale
                total0 = total0 + weight * ak[index, 0]
                total1 = total1 + weight * ak[index, 1]
        return total0, total1

    def edge_sum(slot, first, scale, edges, faces, packed):
        for k in range(1, TERMS):
            at = first + (k - 1) * 2
            along = (tf[at, slot] * scale) * edges[ti[at, slot]] + (tf[at + 1, slot] * scale) * edges[ti[at + 1, slot]]
            packed = faces[k] * along if packed is None else packed + faces[k] * along
        return packed

    def item_copy(j):
        source, target = sb.at[j], rb.at[j, pl.ds(0, 2)] if j < LATE else rl.at[j - LATE, pl.ds(0, 1)]
        if j >= LATE:
            source = sb.at[j, pl.ds(0, 1)]
        return pltpu.make_async_remote_copy(
            source, target, item_s.at[j], item_r.at[j], device_id=partner, device_id_type=MESH
        )

    def inner_copy(n):
        return pltpu.make_async_remote_copy(
            sb.at[LATE + n, pl.ds(1, 1)], rl.at[n, pl.ds(1, 1)], inner_s.at[n], inner_r.at[n],
            device_id=partner, device_id_type=MESH,
        )

    def item_of(j):
        slot = ti[13, j]
        return slot, ti[14, slot], jnp.where(slot // CHIP == high, 1.0, 0.0).astype(f32)

    def slot_at(b):
        return high * CHIP + jnp.where(b < GROUP, core * GROUP + b, (1 - core) * GROUP + b - GROUP)

    def begin_item(j, carry):
        slot, place, ours = item_of(j)
        sb[j, 0], sb[j, 1] = inner_sum(slot, 1.0 - ours, (ours * m[place, 0], ours * m[place, 1]))
        return carry

    def early_item(j):
        slot, place, ours = item_of(j)
        totals = [ours * m[place, 0], ours * m[place, 1]]
        for k in range(1, TERMS):
            at = (k - 1) * 2
            weights = [tf[at + side, slot] * (1.0 - ours) for side in range(2)]
            places = [ti[at + side, slot] for side in range(2)]
            mixed = [weights[0] * m[places[0], p] + weights[1] * m[places[1], p] for p in range(3)]
            def store(_, p, value):
                totals[p] = totals[p] + value
            stencil(mixed, (k,), store)
        sb[j, 0], sb[j, 1] = totals

    for j in range(EARLY):
        early_item(j)
        item_copy(j).start()

    lax.fori_loop(0, CHIP, own_stencil, 0)
    lax.fori_loop(EARLY, EVENS, begin_item, 0)

    for there, side in downs:
        @pl.when(there)
        def _():
            for source in range(2):
                edge_copy(side, 0, source).wait_recv()

    def tile(top0, top1, bottom0, bottom1):
        return jnp.where(row == 0, top0, jnp.where(row == 7, bottom0, jnp.where(row == 4, top1, bottom1)))

    def own_edges(v0, v1):
        return jnp.where(outer, v0, pltpu.roll(v1, 4, 0))

    def arrived(ref, lead, r):
        return [ref[(side,) + lead + (pl.ds(r + p, 1), slice(None))] for side in range(2) for p in range(2)]

    left_out = jnp.logical_or(
        jnp.logical_and(low_seam, upper), jnp.logical_and(high_seam, jnp.logical_or(row == 7, row == 3))
    )
    for k in range(TERMS):
        faces = own_edges(c[k, 0], c[k, 1]) + tile(*arrived(er, (k // 2,), 10 + (k % 2) * 2))
        gh[k] = jnp.where(left_out, 0.0, 0.5 * faces)
    for b in range(CHIP):
        source = core if b < GROUP else 1 - core
        dh[b] = own_edges(m[b, 0], m[b, 1]) - tile(*arrived(er, (source,), (b % GROUP) * 2))

    def merged(one, two):
        which = lax.broadcasted_iota(i32, one.shape, 0)
        stay = (which % 4 == 0) | (which % 4 == 3)
        moved = jnp.where(which % 4 == 1, pltpu.roll(two, 1, 0), pltpu.roll(two, 7, 0))
        return jnp.where(stay, one, moved)

    def second(both):
        which = lax.broadcasted_iota(i32, both.shape, 0)
        return jnp.where(which % 4 == 0, pltpu.roll(both, 7, 0), pltpu.roll(both, 1, 0))

    tile_copy = pltpu.make_async_remote_copy(ts, tr, tile_s, tile_r, device_id=partner, device_id_type=MESH)

    for j in range(EARLY, EVENS):
        slot, place, ours = item_of(j)
        edge0, edge1 = spread(edge_sum(slot, 0, 1.0 - ours, dh, gh, None))
        sb[j, 0] = sb[j, 0] + edge0
        sb[j, 1] = sb[j, 1] + edge1
        if j >= LATE:
            inner_copy(j - LATE).start()
        item_copy(j).start()
        if j == EARLY:
            parts = []
            for n in range(EARLY):
                slot, _, ours = item_of(n)
                packed = edge_sum(slot, 0, 1.0 - ours, dh, gh, None)
                _, place, ours = item_of(LATE + n)
                parts.append(packed + ours * dh[place])
            ts[:, pl.ds(0, width)] = merged(parts[0], parts[1])
            ts[:, pl.ds(width, width // 2)] = merged(parts[2][:, : width // 2], parts[2][:, width // 2 :])
            tile_copy.start()

    def give(n, source, target):
        return pltpu.make_async_remote_copy(
            source, target, give_s.at[n], give_r.at[n], device_id=sibling, device_id_type=MESH
        )

    faces_copy = give(0, gh, ghf)
    tile_on = give(1, tr, trf)
    sums_copy = give(2, acc.at[pl.ds(GROUP, GROUP)], far)
    faces_copy.start()
    lax.fori_loop(0, TERMS, far_faces, 0)

    def local_sum(b, carry):
        slot = slot_at(b)
        weight = tf[13, slot]
        total0, total1 = inner_sum(slot, 1.0, (weight * ak[b * TERMS, 0], weight * ak[b * TERMS, 1]))
        edge0, edge1 = spread(edge_sum(slot, 0, 1.0, dh, gh, gh[0] * (weight * dh[b])))
        acc[b, 0], acc[b, 1] = total0 + edge0, total1 + edge1
        return carry

    lax.fori_loop(0, CHIP, local_sum, 0)

    def plane_copy(j):
        held, at = (rb, j) if j < LATE else (rl, j - LATE)
        return pltpu.make_async_remote_copy(
            held.at[at, pl.ds(1, 1)], held.at[at, pl.ds(2, 1)], plane_s.at[j], plane_r.at[j],
            device_id=sibling, device_id_type=MESH,
        )

    def outer_copy(n):
        return pltpu.make_async_remote_copy(
            rl.at[n, pl.ds(0, 1)], rl.at[n, pl.ds(3, 1)], outer_s.at[n], outer_r.at[n],
            device_id=sibling, device_id_type=MESH,
        )

    def edge_on(side, g):
        return pltpu.make_async_remote_copy(
            hs.at[side, g], hr.at[side, g], fwd_s.at[side, g], fwd_r.at[side, g],
            device_id=(mode, space + (1 if side == 0 else -1)), device_id_type=MESH,
        )

    def raw_stencil(j, carry):
        def store(k, p, value):
            akr[j * 3 + k - 1, p] = value
        stencil((rb[j, 0], rb[j, 1], rb[j, 2]), range(1, TERMS), store)
        return carry

    for g, members in enumerate(groups):
        for n, j in enumerate(members):
            item_copy(j).wait_recv()
            plane_copy(j).start()
            for side, r in ((0, 7), (1, 0)):
                for p in range(2):
                    hs[side, g, pl.ds(n * 2 + p, 1), :] = rb[j, p, pl.ds(r, 1), :]
        for there, side in ups:
            @pl.when(there)
            def _():
                edge_on(side, g).start()
        @pl.when(low_seam)
        def _():
            pl.semaphore_wait(ready, 4)
            for n in range(4):
                seam_copy(1, -1, n, mode).start()

        for j in members:
            plane_copy(j).wait_recv()
        lax.fori_loop(members[0], members[-1] + 1, raw_stencil, 0)
    def remote_sum(b, carry):
        slot = slot_at(b)
        index = ti[12, slot]
        soon = index < LATE
        weight = jnp.where(soon, tf[12, slot], 0.0)
        at = jnp.minimum(index, LATE - 1)
        total0, total1 = acc[b, 0] + weight * rb[at, 0], acc[b, 1] + weight * rb[at, 1]
        for cell in range(6):
            at = ti[6 + cell, slot]
            weight = jnp.where(at < LATE, tf[6 + cell, slot], 0.0)
            at = jnp.minimum(at, LATE - 1) * 3 + cell // 2
            total0 = total0 + weight * akr[at, 0]
            total1 = total1 + weight * akr[at, 1]
        acc[b, 0], acc[b, 1] = total0, total1
        return carry

    lax.fori_loop(0, CHIP, remote_sum, 0)

    def unpack(ref, target):
        target[0] = ref[:, pl.ds(0, width)]
        target[1] = second(ref[:, pl.ds(0, width)])
        target[2, :, pl.ds(0, width // 2)] = ref[:, pl.ds(width, width // 2)]
        target[2, :, pl.ds(width // 2, width // 2)] = second(ref[:, pl.ds(width, width // 2)])

    tile_copy.wait_recv()
    tile_on.start()
    unpack(tr, drl)

    for g, members in enumerate(groups):
        for there, side in downs:
            @pl.when(there)
            def _():
                edge_on(side, g).wait_recv()
        for n, j in enumerate(members):
            dr[j] = own_edges(rb[j, 0], rb[j, 1]) - tile(*arrived(hr, (g,), n * 2))

    def remote_edges(b, carry):
        slot = slot_at(b)
        packed = None
        for k in range(1, TERMS):
            along = None
            for side in range(2):
                cell = 6 + (k - 1) * 2 + side
                at = ti[cell, slot]
                part = jnp.where(at < LATE, tf[cell, slot], 0.0) * dr[jnp.minimum(at, LATE - 1)]
                along = part if along is None else along + part
            packed = gh[k] * along if packed is None else packed + gh[k] * along
        edge0, edge1 = spread(packed)
        acc[b, 0] = acc[b, 0] + edge0
        acc[b, 1] = acc[b, 1] + edge1
        return carry

    lax.fori_loop(0, CHIP, remote_edges, 0)

    def seam_tiles(side, step):
        for source in range(4):
            seam_copy(side, step, 0, source).wait_recv()
        for source in range(2):
            pair_copy(side, 0, source).wait_recv()

        def rows(ref, lead, r):
            return jnp.where(outer, ref[lead, pl.ds(r, 1), :], ref[lead, pl.ds(r + 1, 1), :])

        beside = jnp.logical_or(
            jnp.logical_and(low_seam, upper), jnp.logical_and(high_seam, jnp.logical_or(row == 7, row == 3))
        )
        for k in range(TERMS):
            faces = own_edges(c[k, 0], c[k, 1]) + rows(sh, high * 2 + k // 2, 10 + (k % 2) * 2)
            gs[k] = jnp.where(beside, 0.5 * faces, 0.0)
        for b in range(CHIP):
            source = high * 2 + (core if b < GROUP else 1 - core)
            ds[b] = own_edges(m[b, 0], m[b, 1]) - rows(sh, source, (b % GROUP) * 2)
            ds[CHIP + b] = rows(se, b // GROUP, (b % GROUP) * 2) - rows(sh, (1 - high) * 2 + b // GROUP, (b % GROUP) * 2)

    def seam_sum(b):
        slot = slot_at(b)
        return edge_sum(slot, 16, 1.0, ds, gs, gs[0] * (tf[13, slot] * ds[b]))

    @pl.when(high_seam)
    def _():
        seam_tiles(0, 1)

        def seam_here(b, carry):
            edge0, edge1 = spread(seam_sum(b))
            acc[b, 0] = acc[b, 0] + edge0
            acc[b, 1] = acc[b, 1] + edge1
            return carry

        lax.fori_loop(0, CHIP, seam_here, 0)

    sums_copy.start()

    for n in range(ENDS):
        inner_copy(n).wait_recv()
        plane_copy(LATE + n).start()
        item_copy(LATE + n).wait_recv()
        outer_copy(n).start()

    def late_stencil(far_side, n):
        def store(k, p, value):
            akl[n * 3 + k - 1, p] = value
        near, mid, beyond = (3, 2, 1) if far_side else (0, 1, 2)
        stencil((rl[n, near], rl[n, mid], rl[n, beyond]), range(1, TERMS), store, far_side)

    for n in range(ENDS):
        plane_copy(LATE + n).wait_recv()
        late_stencil(False, n)
        outer_copy(n).wait_recv()
        late_stencil(True, n)
    faces_copy.wait_recv()
    tile_on.wait_recv()
    unpack(trf, drf)
    sums_copy.wait_recv()

    def late_sum(b, carry):
        slot = slot_at(b)
        index = ti[12, slot]
        late = index >= LATE
        weight = jnp.where(late, tf[12, slot], 0.0)
        at = jnp.maximum(index - LATE, 0)
        totals = [acc[b, 0], acc[b, 1], far[b, 1], far[b, 0]]
        totals = [total + weight * rl[at, p] for p, total in enumerate(totals)]
        weight = jnp.where(index < EARLY, tf[12, slot], 0.0)
        at = jnp.minimum(index, EARLY - 1)
        near_edge, far_edge = weight * drl[at], weight * drf[at]
        for n in range(ENDS):
            weight, term = jnp.float32(0.0), jnp.int32(0)
            for cell in range(6):
                found = ti[6 + cell, slot] == LATE + n
                weight = jnp.where(found, tf[6 + cell, slot], weight)
                term = jnp.where(found, cell // 2, term)
            totals = [total + weight * akl[n * 3 + term, p] for p, total in enumerate(totals)]
            near_edge = near_edge + gh[term + 1] * (weight * drl[n])
            far_edge = far_edge + ghf[term + 1] * (weight * drf[n])
        edges = spread(near_edge) + spread(far_edge)[::-1]
        for p in range(4):
            out[b, planes[p]] = totals[p] + edges[p]
        return carry

    lax.fori_loop(0, GROUP, late_sum, 0)

    @pl.when(low_seam)
    def _():
        seam_tiles(1, -1)

        def seam_for_sibling(b, carry):
            sp[b] = seam_sum(b + GROUP)
            return carry

        def seam_for_self(b, carry):
            for plane, edge in zip(planes, spread(seam_sum(b))):
                out[b, plane] = out[b, plane] + edge
            return carry

        def seam_from_sibling(b, carry):
            for plane, edge in zip(planes[::-1], spread(sq[b])):
                out[b, plane] = out[b, plane] + edge
            return carry

        lax.fori_loop(0, GROUP, seam_for_sibling, 0)
        seam_give = give(3, sp, sq)
        seam_give.start()
        lax.fori_loop(0, GROUP, seam_for_self, 0)
        seam_give.wait()
        lax.fori_loop(0, GROUP, seam_from_sibling, 0)

    for copy in to_sibling:
        copy.wait_send()
    for there, side in ups:
        @pl.when(there)
        def _():
            for other in range(2):
                edge_copy(side, other, core).wait_send()
            for g in range(len(groups)):
                edge_on(side, g).wait_send()

    for there, side, step in seams:
        @pl.when(there)
        def _():
            for other in range(2):
                pair_copy(side, other, core).wait_send()
            for n in range(4):
                seam_copy(side, step, n, mode).wait_send()

    for j in range(EVENS):
        item_copy(j).wait_send()
        plane_copy(j).wait_send()
    for n in range(ENDS):
        outer_copy(n).wait_send()
        inner_copy(n).wait_send()
    for copy in (tile_copy, faces_copy, tile_on, sums_copy):
        copy.wait_send()


def galerkin(spaces, modes, coefs, coupling, values, assignment):
    width = modes.shape[3]
    f32 = jnp.float32
    groups = -(-LATE // 4)
    dma = pltpu.SemaphoreType.DMA
    vmem = pltpu.VMEM
    scratch = [
        vmem((CHIP, 4, 8, width), f32),
        vmem((TERMS, 4, 8, width), f32),
        vmem((2, 2, 16, width), f32),
        vmem((2, 2, 16, width), f32),
        vmem((TERMS, 4, 8, width), f32),
        vmem((TERMS, 4, 8, width), f32),
        vmem((TERMS, 4, 8, width), f32),
        vmem((TERMS, 4, 8, width), f32),
        vmem((TERMS, 8, width), f32),
        vmem((CHIP * TERMS, 2, 8, width), f32),
        vmem((CHIP, 8, width), f32),
        vmem((EVENS, 2, 8, width), f32),
        vmem((LATE, 3, 8, width), f32),
        vmem((8, width + width // 2), f32),
        vmem((8, width + width // 2), f32),
        vmem((2, groups, 8, width), f32),
        vmem((2, groups, 8, width), f32),
        vmem((LATE, 8, width), f32),
        vmem((LATE * 3, 2, 8, width), f32),
        vmem((CHIP, 2, 8, width), f32),
        vmem((4, 16, width), f32),
        vmem((2, 16, width), f32),
        vmem((SLOTS, 8, width), f32),
        vmem((TERMS, 8, width), f32),
        vmem((ENDS, 4, 8, width), f32),
        vmem((ENDS * 3, 4, 8, width), f32),
        vmem((EARLY, 8, width), f32),
        vmem((TERMS, 8, width), f32),
        vmem((8, width + width // 2), f32),
        vmem((EARLY, 8, width), f32),
        vmem((GROUP, 2, 8, width), f32),
        vmem((GROUP, 8, width), f32),
        vmem((GROUP, 8, width), f32),
        vmem(coupling.shape, jnp.int32),
        vmem(values.shape, f32),
        vmem(assignment.shape, jnp.int32),
        vmem((24, 128), jnp.int32),
        vmem((24, 128), f32),
        pltpu.SMEM((24, 128), jnp.int32),
        pltpu.SMEM((24, 128), f32),
        dma((2, 4)), dma((3,)), dma((2,)), dma((3,)), dma((3,)), dma((2, 2)), dma((2, 2)), dma((EVENS,)), dma((EVENS,)),
        dma(()), dma(()), dma((EVENS,)), dma((EVENS,)),
        dma((2, groups)), dma((2, groups)), dma((4,)), dma((4,)), dma((2,)), dma((2,)), dma((ENDS,)), dma((ENDS,)),
        dma((4,)), dma((4,)), pltpu.SemaphoreType.REGULAR, dma((ENDS,)), dma((ENDS,)),
    ]
    anywhere = pl.BlockSpec(memory_space=pltpu.HBM)
    return pl.pallas_call(
        functools.partial(kernel, spaces),
        out_shape=jax.ShapeDtypeStruct(modes.shape, f32),
        in_specs=[anywhere] * 5,
        out_specs=pl.BlockSpec(memory_space=pltpu.VMEM),
        scratch_shapes=scratch,
        compiler_params=pltpu.CompilerParams(
            collective_id=0, has_side_effects=True, vmem_limit_bytes=32 * 1024 * 1024
        ),
        name="galerkin",
    )(modes, coefs, coupling, values, assignment)


def solution(mesh):
    spaces = mesh.shape["space"]

    def shards(modes, coefficients, coupling, coupling_values, assignment):
        held = [
            pltpu.with_memory_space_constraint(x, pltpu.HBM)
            for x in (modes, coefficients, coupling.T, coupling_values[None], assignment[None])
        ]
        return galerkin(spaces, *held)

    in_specs = (P("mode", None, "space", None), P(None, None, "space", None), P(), P(), P())
    out_specs = P("mode", None, "space", None)
    return jax.shard_map(shards, mesh=mesh, in_specs=in_specs, out_specs=out_specs, check_vma=False)
```
